256 devices in a mesh: wide: 32 (over y, x, core), narrow: 8 (over z).
Axes of the slice: x: 4, y: 4, z: 8, core: 2. Of those that a mesh axis runs over, the one named last changes fastest.
Arguments:
- queries: bfloat16 [512, 16384], P('wide', 'narrow'), may hold values from -150 to 150
- cache_keys: bfloat16 [512, 256, 1024], P('wide', None, 'narrow'), may hold values from -5 to 5
- cache_values: bfloat16 [512, 256, 1024], P('wide', None, 'narrow'), may hold values from -6 to 6
- new_key: bfloat16 [512, 1024], P('wide', 'narrow'), may hold values from -6 to 6
- new_value: bfloat16 [512, 1024], P('wide', 'narrow'), may hold values from -6 to 6
- lengths: int32 [512], P('wide'), may hold values from 1 to 256, as said below
- out_weight: bfloat16 [16384, 16384], P('narrow', 'wide'), may hold values from -0.046875 to 0.046875
- residual: bfloat16 [512, 16384], P('narrow', 'wide'), may hold values from -30 to 30
- norm_gain: float32 [16384], P('wide'), may hold values from 0.25 to 1.75
- gate_weight: bfloat16 [16384, 26624], P('wide', 'narrow'), may hold values from -0.046875 to 0.046875
- up_weight: bfloat16 [16384, 26624], P('wide', 'narrow'), may hold values from -0.046875 to 0.046875
- down_weight: bfloat16 [26624, 16384], P('narrow', 'wide'), may hold values from -0.0390625 to 0.0390625
Outputs:
- mixed: bfloat16 [512, 16384], P('narrow', 'wide')
The draws below stay inside these ranges and needn't reach their ends.
Inputs may be any that keep to these rules, and one draw needn't show every extreme that they name: `lengths`: some sequence holds exactly 256 cached tokens.
All inputs are finite; a program needn't handle non-finite values.
Results may differ from the reference program's by a relative error of at most 0.007.
Values may be sent and summed in bfloat16 or wider, within the bound.
A program may use at most 128 MiB of HBM per device.

```python
import math
import jax
import jax.numpy as jnp
from jax import lax

D = 16384
H = 128
KV = 8
HD = 128
FFW = 26624
CTX = 256
BATCH = 512


def common_keys(key):
    return jnp.clip(jax.random.normal(key, (BATCH, CTX, KV * HD), jnp.float32), -5.0, 5.0)


def draw_cache_keys(key, part):
    return common_keys(key).astype(jnp.bfloat16)


def draw_queries(key, part):
    key = jax.random.fold_in(key, 11)
    fresh_rows = jnp.clip(jax.random.normal(key, (BATCH, H, HD), jnp.float32), -6.0, 6.0)
    return fresh_rows.reshape(BATCH, H * HD).astype(jnp.bfloat16)


def draw_new_key(key, part):
    key = jax.random.fold_in(key, 13)
    fresh_keys = jnp.clip(jax.random.normal(key, (BATCH, KV * HD), jnp.float32), -5.0, 5.0)
    return fresh_keys.astype(jnp.bfloat16)


def draw_lengths(key, part):
    key = jax.random.fold_in(key, 5)
    first_key, second_key, third_key = jax.random.split(key, 3)
    raw_draw = jax.random.randint(first_key, (BATCH,), 0, CTX)
    shift_count = jax.random.randint(second_key, (BATCH,), 0, 4)
    result = 1 + raw_draw // jnp.left_shift(jnp.ones((BATCH,), jnp.int32), shift_count)
    position = jax.random.randint(third_key, (), 0, BATCH)
    return result.at[position].set(CTX).astype(jnp.int32)


def draw_residual(key, part):
    key = jax.random.fold_in(key, 17)
    first_key = jax.random.fold_in(key, 0)
    column_scale = 0.6 + 1.2 * jnp.arange(D, dtype=jnp.float32) / D
    values = jnp.clip(jax.random.normal(first_key, (BATCH, D), jnp.float32), -6.0, 6.0) * column_scale[None, :]
    return values.astype(jnp.bfloat16)


def levels(stream_key, dims, cuts, least, top_value):
    def one(dim, blocks):
        draws = jax.random.uniform(jax.random.fold_in(jax.random.fold_in(stream_key, 6), dim), (blocks,), jnp.float32, least / len(cuts), top_value / len(cuts))
        return jnp.repeat(jnp.exp(draws), dims[dim] // blocks).reshape((-1,) + (1,) * (len(dims) - dim - 1))

    gain = one(*cuts[0])
    for cut in cuts[1:]:
        gain = gain * one(*cut)
    return gain


def bell_draw(key, shape, deviation, reach, cuts=(), kind=jnp.bfloat16):
    level = levels(key, shape, cuts, -0.22, 0.18) if cuts else 1.0
    values = jax.random.normal(key, shape, jnp.float32) * deviation * level
    return jnp.minimum(jnp.maximum(values, -reach), reach).astype(kind)


def setup_inputs(seed: int = 0) -> dict:
    keys = jax.random.split(jax.random.key(seed), 13)
    queries = draw_queries(jax.random.fold_in(keys[12], 71), 0)
    cache_keys = draw_cache_keys(jax.random.fold_in(keys[12], 71), 0)
    cache_values = bell_draw(keys[2], (BATCH, CTX, KV * HD), 1.0, 6.0, ((0, 32), (2, 8)))
    new_key = draw_new_key(jax.random.fold_in(keys[12], 71), 0)
    new_value = bell_draw(keys[4], (BATCH, KV * HD), 1.0, 6.0, ((0, 32), (1, 8)))
    lengths = draw_lengths(jax.random.fold_in(keys[12], 71), 0)
    out_weight = bell_draw(keys[6], (H * HD, D), (H * HD) ** -0.5, 0.046875, ((0, 8), (1, 32)))
    residual = draw_residual(jax.random.fold_in(keys[12], 71), 0)
    norm_gain = jnp.clip(1.0 + 0.15 * jax.random.normal(keys[8], (D,), jnp.float32), 0.25, 1.75)
    gate_weight = bell_draw(keys[9], (D, FFW), D ** -0.5, 0.046875, ((0, 32), (1, 8)))
    up_weight = bell_draw(keys[10], (D, FFW), D ** -0.5, 0.046875, ((0, 32), (1, 8)))
    down_weight = bell_draw(keys[11], (FFW, D), FFW ** -0.5, 0.0390625, ((0, 8), (1, 32)))
    return dict(queries=queries, cache_keys=cache_keys, cache_values=cache_values, new_key=new_key, new_value=new_value, lengths=lengths, out_weight=out_weight, residual=residual, norm_gain=norm_gain, gate_weight=gate_weight, up_weight=up_weight, down_weight=down_weight)


epsilon = 1e-05

def reference(queries, cache_keys, cache_values, new_key, new_value, lengths, out_weight, residual, norm_gain, gate_weight, up_weight, down_weight):
    group_size = H // KV
    score_scale = 1.0 / math.sqrt(HD)
    query_rows = queries.astype(jnp.float32).reshape(BATCH, KV, group_size, HD)
    key_rows = cache_keys.astype(jnp.float32).reshape(BATCH, CTX, KV, HD)
    value_rows = cache_values.astype(jnp.float32).reshape(BATCH, CTX, KV, HD)
    fresh_key = new_key.astype(jnp.float32).reshape(BATCH, KV, HD)
    fresh_value = new_value.astype(jnp.float32).reshape(BATCH, KV, HD)
    scores = jnp.einsum('sgqd,spgd->sgqp', query_rows, key_rows) * score_scale
    live_mask = jnp.arange(CTX, dtype=jnp.int32)[None, None, None, :] < lengths[:, None, None, None]
    own_score = jnp.einsum('sgqd,sgd->sgq', query_rows, fresh_key) * score_scale
    row_top = jnp.maximum(lax.optimization_barrier(jnp.max(jnp.where(live_mask, scores, -1e+30), axis=-1)), own_score)
    weights_raw = jnp.where(live_mask, jnp.exp(scores - row_top[..., None]), 0.0)
    own_raw = jnp.exp(own_score - row_top)
    row_total = lax.optimization_barrier(jnp.sum(weights_raw, axis=-1)) + own_raw
    weights_bf = (weights_raw / row_total[..., None]).astype(jnp.bfloat16)
    own_bf = (own_raw / row_total).astype(jnp.bfloat16)
    attended = jnp.einsum('sgqp,spgd->sgqd', weights_bf.astype(jnp.float32), value_rows)
    attended = attended + own_bf.astype(jnp.float32)[..., None] * fresh_value[:, :, None, :]
    attended = attended.astype(jnp.bfloat16).reshape(BATCH, H * HD)
    stream = residual.astype(jnp.float32) + jnp.dot(attended, out_weight, preferred_element_type=jnp.float32)
    squares = lax.optimization_barrier(jnp.sum(stream * stream, axis=1, keepdims=True))
    normed = (stream * lax.rsqrt(squares / D + epsilon) * norm_gain).astype(jnp.bfloat16)
    gate = jnp.dot(normed, gate_weight, preferred_element_type=jnp.float32)
    up_part = jnp.dot(normed, up_weight, preferred_element_type=jnp.float32)
    activated = (jax.nn.silu(gate) * up_part).astype(jnp.bfloat16)
    return (stream + jnp.dot(activated, down_weight, preferred_element_type=jnp.float32)).astype(jnp.bfloat16)
```

```python
import functools
import math

import jax
import jax.numpy as jnp
from jax import lax
from jax.experimental import pallas as pl
from jax.experimental.pallas import tpu as pltpu
from jax.sharding import PartitionSpec as P

D = 16384
HD = 128
EPS = 1e-05
NX, NY, NZ = 4, 4, 8
STREAMS = 2
MESH = pl.DeviceIdType.MESH
F32 = jnp.float32
BF16 = jnp.bfloat16


def body(
    len_ref, q_hbm, nk_hbm, nv_hbm, res_hbm, gain_hbm,
    k_hbm, v_hbm, wo_hbm, wg_hbm, wu_hbm, wd_hbm,
    out_ref,
    q_ref, nk_ref, nv_ref, res_ref, gain_ref, kv, vv, wo, wg, wu, wd, gain_sib, qs, ao, ps, pr, ag, po, cs, cr, zs, zr, st,
    xn, sq, gs, gr, gp, gr2, ac, fin,
    lsem, wss, wrs, d2s, d2r, p4s, p4r, zss, zrs,
):
    w = lax.axis_index("wide")
    z = lax.axis_index("narrow")
    c = lax.rem(w, 2)
    chip = lax.div(w, 2)
    x = lax.rem(chip, NX)
    y = lax.div(chip, NX)
    units = wg.shape[1]
    depth = wg.shape[0] // 2

    sibling = (chip * 2 + (1 - c), z)

    p = jnp.where(c == 0, x, y)
    q = jnp.where(c == 0, y, x)

    def natural(second, first):
        return jnp.where(c == 0, second * NX + first, first * NX + second)

    def ppeer(d):
        return lax.rem(p + d, NX)

    def qpeer(d):
        return lax.rem(q + d, NX)

    def zpeer(d):
        return lax.rem(z + d, NZ)

    def pdev(d):
        return (natural(q, ppeer(d)) * 2 + c, z)

    def qdev(d):
        return (natural(qpeer(d), p) * 2 + c, z)

    def zdev(d):
        return (w, zpeer(d))

    barrier = pltpu.get_barrier_semaphore()
    peers = [sibling] + [pdev(d) for d in (1, 2, 3)] + [qdev(d) for d in (1, 2, 3)]
    peers += [zdev(d) for d in range(1, NZ)]
    for dev in peers:
        pl.semaphore_signal(barrier, inc=1, device_id=dev, device_id_type=MESH)

    sent = []
    drained = []

    def send(src, dst, ss, rs, dev):
        copy = pltpu.make_async_remote_copy(
            src_ref=src, dst_ref=dst, send_sem=ss, recv_sem=rs, device_id=dev, device_id_type=MESH
        )
        copy.start()
        sent.append(copy)
        return copy

    def drain(count):
        while len(drained) < count:
            copy = sent[len(drained)]
            copy.wait_send()
            drained.append(copy)

    k_rows = wo.shape[1]
    f_rows = wd.shape[1]
    d_cols = pl.ds(pl.multiple_of(c * units, 128), units)
    d_cols_sib = pl.ds(pl.multiple_of((1 - c) * units, 128), units)
    half = kv.shape[0] // STREAMS
    small = [
        pltpu.make_async_copy(src, dst, lsem.at[8 + i])
        for i, (src, dst) in enumerate((
            (q_hbm, q_ref), (nk_hbm, nk_ref), (nv_hbm, nv_ref), (res_hbm, res_ref),
            (gain_hbm, gain_ref),
        ))
    ]
    loads = []
    for s in range(STREAMS):
        rows = pl.ds(s * half, half)
        loads.append(pltpu.make_async_copy(k_hbm.at[rows], kv.at[rows], lsem.at[2 * s]))
        loads.append(pltpu.make_async_copy(v_hbm.at[rows], vv.at[rows], lsem.at[2 * s + 1]))
    own_rows = pl.ds(pl.multiple_of(c * k_rows, 128), k_rows)
    sib_rows = pl.ds(pl.multiple_of((1 - c) * k_rows, 128), k_rows)
    own_units = pl.ds(pl.multiple_of(c * f_rows, 128), f_rows)
    sib_units = pl.ds(pl.multiple_of((1 - c) * f_rows, 128), f_rows)
    load_wo = pltpu.make_async_copy(wo_hbm.at[own_rows], wo.at[0], lsem.at[4])
    load_wg = pltpu.make_async_copy(wg_hbm.at[:, d_cols], wg.at[0:depth], lsem.at[5])
    load_wu = pltpu.make_async_copy(wu_hbm.at[:, d_cols], wu.at[0:depth], lsem.at[6])
    load_wd = pltpu.make_async_copy(wd_hbm.at[own_units], wd.at[0], lsem.at[7])
    for copy in small + loads + [load_wo, load_wg, load_wu, load_wd]:
        copy.start()

    for copy in small:
        copy.wait()
    heads = q_ref.shape[1] // HD
    seqs = q_ref.shape[0]
    for h in range(heads):
        qs[pl.ds(h, seqs, stride=heads), :] = q_ref[:, h * HD:(h + 1) * HD].astype(F32)

    scale = 1.0 / math.sqrt(HD)

    def attend(s):
        loads[2 * s].wait()
        loads[2 * s + 1].wait()
        ctx = kv.shape[1]
        position = lax.broadcasted_iota(jnp.int32, (heads, ctx), 1)
        items = range(half)
        seq = [s * half + i for i in items]
        query = [qs[n * heads:(n + 1) * heads, :] for n in seq]
        score = [
            lax.dot_general(
                query[i].astype(BF16), kv[seq[i]], (((1,), (1,)), ((), ())),
                preferred_element_type=F32,
            )
            for i in items
        ]
        own = [
            jnp.sum(query[i] * nk_ref[n:n + 1, :].astype(F32), axis=1, keepdims=True) * scale
            for i, n in enumerate(seq)
        ]
        live = [position < len_ref[n] for n in seq]
        score = [jnp.where(live[i], score[i] * scale, -1e30) for i in items]
        top = [jnp.maximum(jnp.max(score[i], axis=1, keepdims=True), own[i]) for i in items]
        raw = [jnp.where(live[i], jnp.exp(score[i] - top[i]), 0.0) for i in items]
        own_raw = [jnp.exp(own[i] - top[i]) for i in items]
        inverse = [1.0 / (jnp.sum(raw[i], axis=1, keepdims=True) + own_raw[i]) for i in items]
        weights = [(raw[i] * inverse[i]).astype(BF16) for i in items]
        own_weight = [(own_raw[i] * inverse[i]).astype(BF16).astype(F32) for i in items]
        mixed = [jnp.dot(weights[i], vv[seq[i]], preferred_element_type=F32) for i in items]
        for i, n in enumerate(seq):
            ao[s, i * heads:(i + 1) * heads, :] = (
                mixed[i] + own_weight[i] * nv_ref[n:n + 1, :].astype(F32)
            )

    per_core = heads // 2

    def swap_start(s):
        for h in range(per_core):
            cols = slice(h * HD, (h + 1) * HD)
            ps[s, 0, :, cols] = ao[s, pl.ds(c * per_core + h, half, stride=heads), :]
            ps[s, 1, :, cols] = ao[s, pl.ds((1 - c) * per_core + h, half, stride=heads), :]
        return send(ps.at[s, 1], pr.at[s], d2s.at[s, 0], d2r.at[s, 0], sibling)

    def gather_first(s, k, buf):
        return [
            send(buf.at[s, q, p], buf.at[s, q, p], p4s.at[s, k, d - 1], p4r.at[s, k, d - 1], pdev(d))
            for d in (2, 1, 3)
        ]

    def gather_second(s, k, buf):
        return [
            send(buf.at[s, q], buf.at[s, q], p4s.at[s, k, d - 1], p4r.at[s, k, d - 1], qdev(d))
            for d in (2, 1, 3)
        ]

    def arrive(copies):
        for copy in copies:
            copy.wait_recv()

    def swap_end_gather(s, copy):
        copy.wait_recv()
        mine = ps[s, 0]
        theirs = pr[s]
        first = jnp.where(c == 0, mine, theirs)
        second = jnp.where(c == 0, theirs, mine)
        block = jnp.concatenate([first, second], axis=0).astype(BF16)
        ag[s, q, p] = block
        return gather_first(s, 0, ag)

    rows = NX * NY * 16

    def project(s, k, buf, weight):
        depth_here = buf.shape[-1]
        for half_index in (1, 0):
            for n in range(weight.shape[-1] // 256):
                cols = slice(n * 256, (n + 1) * 256)
                acc = jnp.dot(buf[s].reshape(rows, depth_here), weight[half_index, :, cols],
                              preferred_element_type=F32)
                for a in range(NY):
                    for b in range(NX):
                        r = (a * NX + b) * 16
                        to = pl.ds(pl.multiple_of(natural(a, b) * 16, 16), 16)
                        if half_index:
                            cs[s, k, to, cols] = acc[r:r + 16].astype(BF16)
                        else:
                            po[s, k, to, cols] = acc[r:r + 16]
            if half_index:
                copy = send(cs.at[s, k], cr.at[s, k], d2s.at[s, 1 + k], d2r.at[s, 1 + k], sibling)
        return copy

    share = rows // NZ

    def scatter_z(s, k, copy):
        copy.wait_recv()
        for j in range(NZ):
            r = slice(j * share, (j + 1) * share)
            zs[s, k, j] = (po[s, k, r, :] + cr[s, k, r, :].astype(F32)).astype(BF16)
        out = []
        for d in (4, 3, 5, 2, 6, 1, 7):
            out.append(send(zs.at[s, k, zpeer(d)], zr.at[s, k, d - 1],
                            zss.at[s, k, d - 1], zrs.at[s, k, d - 1], zdev(d)))
        return out

    def sum_z(s, k, copies):
        own = pl.ds(pl.multiple_of(z * share, share), share)
        acc = po[s, k, own, :] + cr[s, k, own, :].astype(F32)
        arrive(copies)
        for d in range(1, NZ):
            acc += zr[s, k, d - 1].astype(F32)
        return acc

    def norm_gather(s, copies):
        stream = sum_z(s, 0, copies)
        pieces = [
            res_ref[g * 16:(g + 1) * 16, :].astype(F32)[s * 8:(s + 1) * 8] for g in range(share // 8)
        ]
        stream = stream + jnp.concatenate(pieces, axis=0)
        st[s] = stream
        xn[s, z, :, 0:depth] = (stream * gain_ref[...]).astype(BF16)
        out = []
        for d in (4, 3, 5, 2, 6, 1, 7):
            out.append(send(xn.at[s, z, :, 0:depth], xn.at[s, z, :, 0:depth],
                            zss.at[s, 2, d - 1], zrs.at[s, 2, d - 1], zdev(d)))
        return out

    def encode(value):
        high = value.astype(BF16).astype(F32)
        lane = lax.broadcasted_iota(jnp.int32, value.shape, 1)
        return jnp.where(lane < 64, high, value - high).astype(BF16)

    def decode(pair):
        value = pair.astype(F32)
        return value + pltpu.roll(value, 64, 1)

    def row_squares(s, first):
        gain = gain_sib if first else gain_ref
        ungain = 1.0 / gain[...]
        for j in range(NZ):
            value = xn[s, j, :, first:first + depth].astype(F32) * ungain
            value = value * value
            total = value[:, 0:128]
            for n in range(1, depth // 128):
                total += value[:, n * 128:(n + 1) * 128]
            r = slice(j * share, (j + 1) * share)
            if first:
                total += sq[r, :]
                total = jnp.broadcast_to(jnp.sum(total, axis=1, keepdims=True), (share, 128))
            sq[r, :] = total

    def swap_normed(s, copies):
        arrive(copies)
        return send(xn.at[s, :, :, 0:depth], xn.at[s, :, :, depth:2 * depth],
                    d2s.at[s, 3], d2r.at[s, 3], sibling)

    def spread(s, cols, value):
        for j in range(NY):
            for i in range(NX):
                r = (j * NX + i) * 16
                first = jnp.where(c == 0, i, j)
                second = jnp.where(c == 0, j, i)
                gs[s, first, second, :, cols] = value[r:r + 16]

    def expand(s, copy):
        row_squares(s, 0)
        copy.wait_recv()
        row_squares(s, depth)
        spread(s, slice(2 * units, 2 * units + 128), encode(sq[...]))
        for k, weight in enumerate((wg, wu)):
            for start in range(0, units, 256):
                size = min(256, units - start)
                acc = jnp.dot(xn[s].reshape(rows, 2 * depth), weight[:, start:start + size],
                              preferred_element_type=F32)
                base = k * units + start
                spread(s, slice(base, base + size), acc.astype(BF16))
        return [
            send(gs.at[s, ppeer(d)], gr.at[s, d - 1], p4s.at[s, 2, d - 1], p4r.at[s, 2, d - 1],
                 pdev(d))
            for d in (2, 1, 3)
        ]

    def sum_second(s, copies):
        arrive(copies)

        def block(j, _):
            acc = gs[s, p, j, :, 0:2 * units].astype(F32)
            square = decode(gs[s, p, j, :, 2 * units:])
            for d in range(3):
                acc += gr[s, d, j, :, 0:2 * units].astype(F32)
                square += decode(gr[s, d, j, :, 2 * units:])
            gp[s, j, :, 0:2 * units] = acc.astype(BF16)
            gp[s, j, :, 2 * units:] = encode(square)
            return 0
        lax.fori_loop(0, NY, block, 0)
        return [
            send(gp.at[s, qpeer(d)], gr2.at[s, d - 1], p4s.at[s, 3, d - 1], p4r.at[s, 3, d - 1],
                 qdev(d))
            for d in (2, 1, 3)
        ]

    def activate(s, copies):
        arrive(copies)
        square = decode(gp[s, q, :, 2 * units:])
        for d in range(3):
            square += decode(gr2[s, d, :, 2 * units:])
        factor = lax.rsqrt(square / D + EPS)
        for n in range(units // 128):
            cols = slice(n * 128, (n + 1) * 128)
            lift_cols = slice(units + n * 128, units + (n + 1) * 128)
            gate = gp[s, q, :, cols].astype(F32)
            lift = gp[s, q, :, lift_cols].astype(F32)
            for d in range(3):
                gate += gr2[s, d, :, cols].astype(F32)
                lift += gr2[s, d, :, lift_cols].astype(F32)
            gate = gate * factor
            ac[s, q, p, :, cols] = (
                gate / (1.0 + jnp.exp(-gate)) * (lift * factor)
            ).astype(BF16)
        return gather_first(s, 4, ac)

    S = range(STREAMS)
    for s in S:
        attend(s)
    pl.semaphore_wait(barrier, len(peers))
    swaps = [swap_start(s) for s in S]
    share_gain = send(gain_hbm, gain_sib, wss.at[4], wrs.at[4], sibling)
    share_wo = send(wo_hbm.at[sib_rows], wo.at[1], wss.at[0], wrs.at[0], sibling)
    a1 = [swap_end_gather(s, swaps[s]) for s in S]
    share_wg = send(wg_hbm.at[:, d_cols_sib], wg.at[depth:2 * depth], wss.at[1], wrs.at[1], sibling)
    share_wu = send(wu_hbm.at[:, d_cols_sib], wu.at[depth:2 * depth], wss.at[2], wrs.at[2], sibling)
    a2 = []
    for s in S:
        arrive(a1[s])
        a2.append(gather_second(s, 1, ag))
    load_wo.wait()
    share_wo.wait_recv()
    r1 = []
    for s in S:
        arrive(a2[s])
        c1 = project(s, 0, ag, wo)
        r1.append(scatter_z(s, 0, c1))
    share_wd = send(wd_hbm.at[sib_units], wd.at[1], wss.at[3], wrs.at[3], sibling)
    for copy in (load_wg, load_wu, load_wd):
        copy.wait()
    for copy in (share_gain, share_wg, share_wu):
        copy.wait_recv()
    drain(16)
    n1 = [norm_gather(s, r1[s]) for s in S]
    drain(32)
    share_wd.wait_recv()
    e1 = []
    for s in S:
        e1.append(expand(s, swap_normed(s, n1[s])))
    drain(48)
    e2 = [sum_second(0, e1[0])]
    b1 = [activate(0, e2[0])]
    e2.append(sum_second(1, e1[1]))
    arrive(b1[0])
    b2 = [gather_second(0, 5, ac)]
    b1.append(activate(1, e2[1]))
    arrive(b2[0])
    c2 = project(0, 1, ac, wd)
    arrive(b1[1])
    b2.append(gather_second(1, 5, ac))
    r2 = [scatter_z(0, 1, c2)]
    drain(len(sent) - 24)
    arrive(b2[1])
    c2 = project(1, 1, ac, wd)
    r2.append(scatter_z(1, 1, c2))
    drain(len(sent) - 9)
    for s in S:
        fin[s] = st[s] + sum_z(s, 1, r2[s])
    for g in range(share // 8):
        out_ref[g * 16:(g + 1) * 16, :] = jnp.concatenate(
            [fin[s, g * 8:(g + 1) * 8, :] for s in S], axis=0
        ).astype(BF16)
    drain(len(sent))


def local(
    queries, cache_keys, cache_values, new_key, new_value, lengths,
    out_weight, residual, norm_gain, gate_weight, up_weight, down_weight,
):
    seqs, ctx, _ = cache_keys.shape
    heads = queries.shape[1] // HD
    half = seqs // STREAMS
    kh = out_weight.shape[0] // 2
    cols = out_weight.shape[1]
    depth, hidden = gate_weight.shape
    units = hidden // 2
    wide_row = 2 * units + 128
    rows = NX * NY * 2 * half
    share = rows // NZ
    S = STREAMS
    DMA = pltpu.SemaphoreType.DMA

    def v(*shape, dtype=BF16):
        return pltpu.VMEM(shape, dtype)

    scratch = [
        v(*queries.shape), v(*new_key.shape), v(*new_value.shape), v(*residual.shape),
        v(1, cols, dtype=F32),
        v(seqs, ctx, HD), v(seqs, ctx, HD),
        v(2, kh, cols), v(2 * depth, units), v(2 * depth, units), v(2, units, cols),
        v(1, cols, dtype=F32),
        v(seqs * heads, HD, dtype=F32),
        v(S, half * heads, HD, dtype=F32),
        v(S, 2, half, kh, dtype=F32), v(S, half, kh, dtype=F32),
        v(S, NY, NX, 16, kh),
        v(S, 2, rows, cols, dtype=F32),
        v(S, 2, rows, cols), v(S, 2, rows, cols),
        v(S, 2, NZ, share, cols), v(S, 2, NZ - 1, share, cols),
        v(S, share, cols, dtype=F32),
        v(S, NZ, share, 2 * depth), v(rows, 128, dtype=F32),
        v(S, NX, NY, 16, wide_row), v(S, 3, NY, 16, wide_row),
        v(S, NY, 16, wide_row), v(S, 3, 16, wide_row),
        v(S, NY, NX, 16, units),
        v(S, share, cols, dtype=F32),
        DMA((13,)), DMA((5,)), DMA((5,)),
        DMA((S, 4)), DMA((S, 4)),
        DMA((S, 6, 3)), DMA((S, 6, 3)),
        DMA((S, 3, NZ - 1)), DMA((S, 3, NZ - 1)),
    ]
    vm = pl.BlockSpec(memory_space=pltpu.VMEM)
    hbm = pl.BlockSpec(memory_space=pl.ANY)
    return pl.pallas_call(
        body,
        out_shape=jax.ShapeDtypeStruct(residual.shape, BF16),
        in_specs=[pl.BlockSpec(memory_space=pltpu.SMEM)] + [hbm] * 11,
        out_specs=vm,
        scratch_shapes=scratch,
        compiler_params=pltpu.CompilerParams(
            collective_id=0, has_side_effects=True, vmem_limit_bytes=58 << 20
        ),
        name="layer",
    )(
        lengths, queries, new_key, new_value, residual, norm_gain.reshape(1, -1),
        cache_keys, cache_values, out_weight, gate_weight, up_weight, down_weight,
    )


def solution(mesh):
    in_specs = (
        P("wide", "narrow"),
        P("wide", None, "narrow"),
        P("wide", None, "narrow"),
        P("wide", "narrow"),
        P("wide", "narrow"),
        P("wide"),
        P("narrow", "wide"),
        P("narrow", "wide"),
        P("wide"),
        P("wide", "narrow"),
        P("wide", "narrow"),
        P("narrow", "wide"),
    )
    out_specs = P("narrow", "wide")
    return jax.shard_map(local, mesh=mesh, in_specs=in_specs, out_specs=out_specs, check_vma=False)
```

```python
import functools
import math

import jax
import jax.numpy as jnp
from jax import lax
from jax.experimental import pallas as pl
from jax.experimental.pallas import tpu as pltpu
from jax.sharding import PartitionSpec as P

D = 16384
HD = 128
EPS = 1e-05
NX, NY, NZ = 4, 4, 8
STREAMS = 2
MESH = pl.DeviceIdType.MESH
F32 = jnp.float32
BF16 = jnp.bfloat16


def body(
    len_ref, q_hbm, nk_hbm, nv_hbm, res_hbm, gain_hbm,
    k_hbm, v_hbm, wo_hbm, wg_hbm, wu_hbm, wd_hbm,
    out_ref,
    q_ref, nk_ref, nv_ref, res_ref, gain_ref, kv, vv, wo, wg, wu, wd, gain_sib, qs, ao, ps, pr, ag, po, cs, cr, zs, zr, zt, st,
    xn, sq, gs, gr, gp, gr2, ac, fin,
    lsem, wss, wrs, d2s, d2r, p4s, p4r, zss, zrs,
):
    w = lax.axis_index("wide")
    z = lax.axis_index("narrow")
    c = lax.rem(w, 2)
    chip = lax.div(w, 2)
    x = lax.rem(chip, NX)
    y = lax.div(chip, NX)
    units = wg.shape[1]
    depth = wg.shape[0] // 2

    sibling = (chip * 2 + (1 - c), z)

    p = jnp.where(c == 0, x, y)
    q = jnp.where(c == 0, y, x)

    def natural(second, first):
        return jnp.where(c == 0, second * NX + first, first * NX + second)

    def ppeer(d):
        return lax.rem(p + d, NX)

    def qpeer(d):
        return lax.rem(q + d, NX)

    def zpeer(d):
        return lax.rem(z + d, NZ)

    def pdev(d):
        return (natural(q, ppeer(d)) * 2 + c, z)

    def qdev(d):
        return (natural(qpeer(d), p) * 2 + c, z)

    def zdev(d):
        return (w, zpeer(d))

    barrier = pltpu.get_barrier_semaphore()
    peers = [sibling] + [pdev(d) for d in (1, 2, 3)] + [qdev(d) for d in (1, 2, 3)]
    peers += [zdev(d) for d in range(1, NZ)]
    for dev in peers:
        pl.semaphore_signal(barrier, inc=1, device_id=dev, device_id_type=MESH)

    sent = []
    drained = []

    def send(src, dst, ss, rs, dev):
        copy = pltpu.make_async_remote_copy(
            src_ref=src, dst_ref=dst, send_sem=ss, recv_sem=rs, device_id=dev, device_id_type=MESH
        )
        copy.start()
        sent.append(copy)
        return copy

    def drain(count):
        while len(drained) < count:
            copy = sent[len(drained)]
            copy.wait_send()
            drained.append(copy)

    k_rows = wo.shape[1]
    f_rows = wd.shape[1]
    d_cols = pl.ds(pl.multiple_of(c * units, 128), units)
    d_cols_sib = pl.ds(pl.multiple_of((1 - c) * units, 128), units)
    half = kv.shape[0] // STREAMS
    small = [
        pltpu.make_async_copy(src, dst, lsem.at[8 + i])
        for i, (src, dst) in enumerate((
            (q_hbm, q_ref), (nk_hbm, nk_ref), (nv_hbm, nv_ref), (res_hbm, res_ref),
            (gain_hbm, gain_ref),
        ))
    ]
    loads = []
    for s in range(STREAMS):
        rows = pl.ds(s * half, half)
        loads.append(pltpu.make_async_copy(k_hbm.at[rows], kv.at[rows], lsem.at[2 * s]))
        loads.append(pltpu.make_async_copy(v_hbm.at[rows], vv.at[rows], lsem.at[2 * s + 1]))
    own_rows = pl.ds(pl.multiple_of(c * k_rows, 128), k_rows)
    sib_rows = pl.ds(pl.multiple_of((1 - c) * k_rows, 128), k_rows)
    own_units = pl.ds(pl.multiple_of(c * f_rows, 128), f_rows)
    sib_units = pl.ds(pl.multiple_of((1 - c) * f_rows, 128), f_rows)
    load_wo = pltpu.make_async_copy(wo_hbm.at[own_rows], wo.at[0], lsem.at[4])
    load_wg = pltpu.make_async_copy(wg_hbm.at[:, d_cols], wg.at[0:depth], lsem.at[5])
    load_wu = pltpu.make_async_copy(wu_hbm.at[:, d_cols], wu.at[0:depth], lsem.at[6])
    load_wd = pltpu.make_async_copy(wd_hbm.at[own_units], wd.at[0], lsem.at[7])
    for copy in small + loads + [load_wo, load_wg, load_wu, load_wd]:
        copy.start()

    for copy in small:
        copy.wait()
    heads = q_ref.shape[1] // HD
    seqs = q_ref.shape[0]
    for h in range(heads):
        qs[pl.ds(h, seqs, stride=heads), :] = q_ref[:, h * HD:(h + 1) * HD].astype(F32)

    scale = 1.0 / math.sqrt(HD)

    def attend(s):
        loads[2 * s].wait()
        loads[2 * s + 1].wait()
        ctx = kv.shape[1]
        position = lax.broadcasted_iota(jnp.int32, (heads, ctx), 1)
        items = range(half)
        seq = [s * half + i for i in items]
        query = [qs[n * heads:(n + 1) * heads, :] for n in seq]
        score = [
            lax.dot_general(
                query[i].astype(BF16), kv[seq[i]], (((1,), (1,)), ((), ())),
                preferred_element_type=F32,
            )
            for i in items
        ]
        own = [
            jnp.sum(query[i] * nk_ref[n:n + 1, :].astype(F32), axis=1, keepdims=True) * scale
            for i, n in enumerate(seq)
        ]
        live = [position < len_ref[n] for n in seq]
        score = [jnp.where(live[i], score[i] * scale, -1e30) for i in items]
        top = [jnp.maximum(jnp.max(score[i], axis=1, keepdims=True), own[i]) for i in items]
        raw = [jnp.where(live[i], jnp.exp(score[i] - top[i]), 0.0) for i in items]
        own_raw = [jnp.exp(own[i] - top[i]) for i in items]
        inverse = [1.0 / (jnp.sum(raw[i], axis=1, keepdims=True) + own_raw[i]) for i in items]
        weights = [(raw[i] * inverse[i]).astype(BF16) for i in items]
        own_weight = [(own_raw[i] * inverse[i]).astype(BF16).astype(F32) for i in items]
        mixed = [jnp.dot(weights[i], vv[seq[i]], preferred_element_type=F32) for i in items]
        for i, n in enumerate(seq):
            ao[s, i * heads:(i + 1) * heads, :] = (
                mixed[i] + own_weight[i] * nv_ref[n:n + 1, :].astype(F32)
            )

    per_core = heads // 2

    def swap_start(s):
        for h in range(per_core):
            cols = slice(h * HD, (h + 1) * HD)
            ps[s, 0, :, cols] = ao[s, pl.ds(c * per_core + h, half, stride=heads), :]
            ps[s, 1, :, cols] = ao[s, pl.ds((1 - c) * per_core + h, half, stride=heads), :]
        return send(ps.at[s, 1], pr.at[s], d2s.at[s, 0], d2r.at[s, 0], sibling)

    def gather_first(s, k, buf):
        return [
            send(buf.at[s, q, p], buf.at[s, q, p], p4s.at[s, k, d - 1], p4r.at[s, k, d - 1], pdev(d))
            for d in (2, 1, 3)
        ]

    def gather_second(s, k, buf):
        return [
            send(buf.at[s, q], buf.at[s, q], p4s.at[s, k, d - 1], p4r.at[s, k, d - 1], qdev(d))
            for d in (2, 1, 3)
        ]

    def arrive(copies):
        for copy in copies:
            copy.wait_recv()

    def swap_end_gather(s, copy):
        copy.wait_recv()
        mine = ps[s, 0]
        theirs = pr[s]
        first = jnp.where(c == 0, mine, theirs)
        second = jnp.where(c == 0, theirs, mine)
        block = jnp.concatenate([first, second], axis=0).astype(BF16)
        ag[s, q, p] = block
        return gather_first(s, 0, ag)

    rows = NX * NY * 16

    def project(s, k, buf, weight):
        depth_here = buf.shape[-1]
        for half_index in (1, 0):
            for n in range(weight.shape[-1] // 256):
                cols = slice(n * 256, (n + 1) * 256)
                acc = jnp.dot(buf[s].reshape(rows, depth_here), weight[half_index, :, cols],
                              preferred_element_type=F32)
                for a in range(NY):
                    for b in range(NX):
                        r = (a * NX + b) * 16
                        to = pl.ds(pl.multiple_of(natural(a, b) * 16, 16), 16)
                        if half_index:
                            cs[s, k, to, cols] = acc[r:r + 16].astype(BF16)
                        else:
                            po[s, k, to, cols] = acc[r:r + 16]
            if half_index:
                copy = send(cs.at[s, k], cr.at[s, k], d2s.at[s, 1 + k], d2r.at[s, 1 + k], sibling)
        return copy

    share = rows // NZ

    top, bottom = slice(0, share // 2), slice(share // 2, share)

    def zsend(s, k, i, src, dst, d):
        return send(src, dst, zss.at[s, k, i], zrs.at[s, k, i], zdev(d))

    def scatter_z(s, k, copy):
        copy.wait_recv()
        for j in range(NZ):
            r = slice(j * share, (j + 1) * share)
            zs[s, k, j] = (po[s, k, r, :] + cr[s, k, r, :].astype(F32)).astype(BF16)
        src = [zs.at[s, k, zpeer(d)] for d in range(NZ)]
        return [
            zsend(s, k, 0, src[4].at[top], zr.at[s, k, 0, top], 2),
            zsend(s, k, 1, src[4].at[bottom], zr.at[s, k, 1, bottom], 6),
            zsend(s, k, 2, src[3], zr.at[s, k, 2], 1),
            zsend(s, k, 3, src[5], zr.at[s, k, 3], 7),
            zsend(s, k, 4, src[1], zr.at[s, k, 4], 1),
            zsend(s, k, 5, src[7], zr.at[s, k, 5], 7),
        ]

    def relay_z(s, k, copies):
        for i, (part, d) in enumerate(((top, 2), (bottom, 6))):
            copies[i].wait_recv()
            copies[2 + i].wait_recv()
            to = zpeer(d)
            zt[s, k, i] = (zs[s, k, to].astype(F32) + zr[s, k, 2 + i].astype(F32)).astype(BF16)
            zt[s, k, i, part] = (
                zs[s, k, to, part].astype(F32) + zr[s, k, 2 + i, part].astype(F32)
                + zr[s, k, i, part].astype(F32)
            ).astype(BF16)
            copies.append(zsend(s, k, 6 + i, zt.at[s, k, i], zr.at[s, k, 6 + i], d))
        return copies[4:]

    def sum_z(s, k, copies):
        own = pl.ds(pl.multiple_of(z * share, share), share)
        acc = po[s, k, own, :] + cr[s, k, own, :].astype(F32)
        arrive(copies)
        for i in range(4, 8):
            acc += zr[s, k, i].astype(F32)
        return acc

    def norm_gather(s, copies):
        stream = sum_z(s, 0, copies)
        pieces = [
            res_ref[g * 16:(g + 1) * 16, :].astype(F32)[s * 8:(s + 1) * 8] for g in range(share // 8)
        ]
        stream = stream + jnp.concatenate(pieces, axis=0)
        st[s] = stream
        xn[s, z, :, 0:depth] = (stream * gain_ref[...]).astype(BF16)
        block = xn.at[s, z, :, 0:depth]
        return [zsend(s, 2, i, block, block, d) for i, d in enumerate((2, 6, 1, 7))]

    def relay_normed(s, copies):
        for i, (part, near, far) in enumerate(((top, 1, 2), (bottom, 7, 6))):
            copies[i].wait_recv()
            came = zpeer(NZ - far)
            half_block = xn.at[s, came, part, 0:depth]
            block = xn.at[s, came, :, 0:depth]
            copies.append(zsend(s, 2, 4 + 2 * i, half_block, half_block, far))
            copies.append(zsend(s, 2, 5 + 2 * i, block, block, near))
        return copies[2:]

    def encode(value):
        high = value.astype(BF16).astype(F32)
        lane = lax.broadcasted_iota(jnp.int32, value.shape, 1)
        return jnp.where(lane < 64, high, value - high).astype(BF16)

    def decode(pair):
        value = pair.astype(F32)
        return value + pltpu.roll(value, 64, 1)

    def row_squares(s, first):
        gain = gain_sib if first else gain_ref
        ungain = 1.0 / gain[...]
        for j in range(NZ):
            value = xn[s, j, :, first:first + depth].astype(F32) * ungain
            value = value * value
            total = value[:, 0:128]
            for n in range(1, depth // 128):
                total += value[:, n * 128:(n + 1) * 128]
            r = slice(j * share, (j + 1) * share)
            if first:
                total += sq[r, :]
                total = jnp.broadcast_to(jnp.sum(total, axis=1, keepdims=True), (share, 128))
            sq[r, :] = total

    def swap_normed(s, copies):
        arrive(copies)
        return send(xn.at[s, :, :, 0:depth], xn.at[s, :, :, depth:2 * depth],
                    d2s.at[s, 3], d2r.at[s, 3], sibling)

    def spread(s, cols, value):
        for j in range(NY):
            for i in range(NX):
                r = (j * NX + i) * 16
                first = jnp.where(c == 0, i, j)
                second = jnp.where(c == 0, j, i)
                gs[s, first, second, :, cols] = value[r:r + 16]

    def expand(s, copy):
        row_squares(s, 0)
        copy.wait_recv()
        row_squares(s, depth)
        spread(s, slice(2 * units, 2 * units + 128), encode(sq[...]))
        for k, weight in enumerate((wg, wu)):
            for start in range(0, units, 256):
                size = min(256, units - start)
                acc = jnp.dot(xn[s].reshape(rows, 2 * depth), weight[:, start:start + size],
                              preferred_element_type=F32)
                base = k * units + start
                spread(s, slice(base, base + size), acc.astype(BF16))
        return [
            send(gs.at[s, ppeer(d)], gr.at[s, d - 1], p4s.at[s, 2, d - 1], p4r.at[s, 2, d - 1],
                 pdev(d))
            for d in (2, 1, 3)
        ]

    def sum_second(s, copies):
        arrive(copies)

        def block(j, _):
            acc = gs[s, p, j, :, 0:2 * units].astype(F32)
            square = decode(gs[s, p, j, :, 2 * units:])
            for d in range(3):
                acc += gr[s, d, j, :, 0:2 * units].astype(F32)
                square += decode(gr[s, d, j, :, 2 * units:])
            gp[s, j, :, 0:2 * units] = acc.astype(BF16)
            gp[s, j, :, 2 * units:] = encode(square)
            return 0
        lax.fori_loop(0, NY, block, 0)
        return [
            send(gp.at[s, qpeer(d)], gr2.at[s, d - 1], p4s.at[s, 3, d - 1], p4r.at[s, 3, d - 1],
                 qdev(d))
            for d in (2, 1, 3)
        ]

    def activate(s, copies):
        arrive(copies)
        square = decode(gp[s, q, :, 2 * units:])
        for d in range(3):
            square += decode(gr2[s, d, :, 2 * units:])
        factor = lax.rsqrt(square / D + EPS)
        for n in range(units // 128):
            cols = slice(n * 128, (n + 1) * 128)
            lift_cols = slice(units + n * 128, units + (n + 1) * 128)
            gate = gp[s, q, :, cols].astype(F32)
            lift = gp[s, q, :, lift_cols].astype(F32)
            for d in range(3):
                gate += gr2[s, d, :, cols].astype(F32)
                lift += gr2[s, d, :, lift_cols].astype(F32)
            gate = gate * factor
            ac[s, q, p, :, cols] = (
                gate / (1.0 + jnp.exp(-gate)) * (lift * factor)
            ).astype(BF16)
        return gather_first(s, 4, ac)

    S = range(STREAMS)
    for s in S:
        attend(s)
    pl.semaphore_wait(barrier, len(peers))
    swaps = [swap_start(s) for s in S]
    share_gain = send(gain_hbm, gain_sib, wss.at[4], wrs.at[4], sibling)
    share_wo = send(wo_hbm.at[sib_rows], wo.at[1], wss.at[0], wrs.at[0], sibling)
    a1 = [swap_end_gather(s, swaps[s]) for s in S]
    share_wg = send(wg_hbm.at[:, d_cols_sib], wg.at[depth:2 * depth], wss.at[1], wrs.at[1], sibling)
    share_wu = send(wu_hbm.at[:, d_cols_sib], wu.at[depth:2 * depth], wss.at[2], wrs.at[2], sibling)
    a2 = []
    for s in S:
        arrive(a1[s])
        a2.append(gather_second(s, 1, ag))
    load_wo.wait()
    share_wo.wait_recv()
    r1 = []
    for s in S:
        arrive(a2[s])
        c1 = project(s, 0, ag, wo)
        r1.append(scatter_z(s, 0, c1))
    share_wd = send(wd_hbm.at[sib_units], wd.at[1], wss.at[3], wrs.at[3], sibling)
    for copy in (load_wg, load_wu, load_wd):
        copy.wait()
    for copy in (share_gain, share_wg, share_wu):
        copy.wait_recv()
    drain(16)
    r1 = [relay_z(s, 0, r1[s]) for s in S]
    n1 = [norm_gather(s, r1[s]) for s in S]
    n1 = [relay_normed(s, n1[s]) for s in S]
    drain(32)
    share_wd.wait_recv()
    e1 = []
    for s in S:
        e1.append(expand(s, swap_normed(s, n1[s])))
    drain(48)
    e2 = [sum_second(0, e1[0])]
    b1 = [activate(0, e2[0])]
    e2.append(sum_second(1, e1[1]))
    arrive(b1[0])
    b2 = [gather_second(0, 5, ac)]
    b1.append(activate(1, e2[1]))
    arrive(b2[0])
    c2 = project(0, 1, ac, wd)
    arrive(b1[1])
    b2.append(gather_second(1, 5, ac))
    r2 = [scatter_z(0, 1, c2)]
    drain(len(sent) - 24)
    arrive(b2[1])
    c2 = project(1, 1, ac, wd)
    r2[0] = relay_z(0, 1, r2[0])
    r2.append(scatter_z(1, 1, c2))
    drain(len(sent) - 16)
    r2[1] = relay_z(1, 1, r2[1])
    for s in S:
        fin[s] = st[s] + sum_z(s, 1, r2[s])
    for g in range(share // 8):
        out_ref[g * 16:(g + 1) * 16, :] = jnp.concatenate(
            [fin[s, g * 8:(g + 1) * 8, :] for s in S], axis=0
        ).astype(BF16)
    drain(len(sent))


def local(
    queries, cache_keys, cache_values, new_key, new_value, lengths,
    out_weight, residual, norm_gain, gate_weight, up_weight, down_weight,
):
    seqs, ctx, _ = cache_keys.shape
    heads = queries.shape[1] // HD
    half = seqs // STREAMS
    kh = out_weight.shape[0] // 2
    cols = out_weight.shape[1]
    depth, hidden = gate_weight.shape
    units = hidden // 2
    wide_row = 2 * units + 128
    rows = NX * NY * 2 * half
    share = rows // NZ
    S = STREAMS
    DMA = pltpu.SemaphoreType.DMA

    def v(*shape, dtype=BF16):
        return pltpu.VMEM(shape, dtype)

    scratch = [
        v(*queries.shape), v(*new_key.shape), v(*new_value.shape), v(*residual.shape),
        v(1, cols, dtype=F32),
        v(seqs, ctx, HD), v(seqs, ctx, HD),
        v(2, kh, cols), v(2 * depth, units), v(2 * depth, units), v(2, units, cols),
        v(1, cols, dtype=F32),
        v(seqs * heads, HD, dtype=F32),
        v(S, half * heads, HD, dtype=F32),
        v(S, 2, half, kh, dtype=F32), v(S, half, kh, dtype=F32),
        v(S, NY, NX, 16, kh),
        v(S, 2, rows, cols, dtype=F32),
        v(S, 2, rows, cols), v(S, 2, rows, cols),
        v(S, 2, NZ, share, cols), v(S, 2, 8, share, cols),
        v(S, 2, 2, share, cols),
        v(S, share, cols, dtype=F32),
        v(S, NZ, share, 2 * depth), v(rows, 128, dtype=F32),
        v(S, NX, NY, 16, wide_row), v(S, 3, NY, 16, wide_row),
        v(S, NY, 16, wide_row), v(S, 3, 16, wide_row),
        v(S, NY, NX, 16, units),
        v(S, share, cols, dtype=F32),
        DMA((13,)), DMA((5,)), DMA((5,)),
        DMA((S, 4)), DMA((S, 4)),
        DMA((S, 6, 3)), DMA((S, 6, 3)),
        DMA((S, 3, 8)), DMA((S, 3, 8)),
    ]
    vm = pl.BlockSpec(memory_space=pltpu.VMEM)
    hbm = pl.BlockSpec(memory_space=pl.ANY)
    return pl.pallas_call(
        body,
        out_shape=jax.ShapeDtypeStruct(residual.shape, BF16),
        in_specs=[pl.BlockSpec(memory_space=pltpu.SMEM)] + [hbm] * 11,
        out_specs=vm,
        scratch_shapes=scratch,
        compiler_params=pltpu.CompilerParams(
            collective_id=0, has_side_effects=True, vmem_limit_bytes=58 << 20
        ),
        name="layer",
    )(
        lengths, queries, new_key, new_value, residual, norm_gain.reshape(1, -1),
        cache_keys, cache_values, out_weight, gate_weight, up_weight, down_weight,
    )


def solution(mesh):
    in_specs = (
        P("wide", "narrow"),
        P("wide", None, "narrow"),
        P("wide", None, "narrow"),
        P("wide", "narrow"),
        P("wide", "narrow"),
        P("wide"),
        P("narrow", "wide"),
        P("narrow", "wide"),
        P("wide"),
        P("wide", "narrow"),
        P("wide", "narrow"),
        P("narrow", "wide"),
    )
    out_specs = P("narrow", "wide")
    return jax.shard_map(local, mesh=mesh, in_specs=in_specs, out_specs=out_specs, check_vma=False)
```

```python
import functools
import math

import jax
import jax.numpy as jnp
from jax import lax
from jax.experimental import pallas as pl
from jax.experimental.pallas import tpu as pltpu
from jax.sharding import PartitionSpec as P

D = 16384
HD = 128
EPS = 1e-05
NX, NY, NZ = 4, 4, 8
STREAMS = 2
MESH = pl.DeviceIdType.MESH
F32 = jnp.float32
BF16 = jnp.bfloat16


def body(
    len_ref, q_hbm, nk_hbm, nv_hbm, res_hbm, gain_hbm,
    k_hbm, v_hbm, wo_hbm, wg_hbm, wu_hbm, wd_hbm,
    out_ref,
    q_ref, nk_ref, nv_ref, res_ref, gain_ref, kv, vv, wo, wg, wu, wd, gain_sib, qs, ao, ps, pr, ag, po, cs, cr, zs, zr, zt, st,
    xn, sq, ga0, ga1, gb0, gb1, ra0, ra1, rb0, rb1, ha0, ha1, hb0, hb1, gp0, gp1, gr20, gr21, ac0, ac1, psum, scales, fin,
    lsem, wss, wrs, d2s, d2r, p4s, p4r, zss, zrs,
):
    ga, gb, ra, rb = (ga0, ga1), (gb0, gb1), (ra0, ra1), (rb0, rb1)
    ha, hb, gp, gr2, ac = (ha0, ha1), (hb0, hb1), (gp0, gp1), (gr20, gr21), (ac0, ac1)
    w = lax.axis_index("wide")
    z = lax.axis_index("narrow")
    c = lax.rem(w, 2)
    chip = lax.div(w, 2)
    x = lax.rem(chip, NX)
    y = lax.div(chip, NX)
    units = wg.shape[1]
    depth = wg.shape[0] // 2

    sibling = (chip * 2 + (1 - c), z)

    p = jnp.where(c == 0, x, y)
    q = jnp.where(c == 0, y, x)

    def natural(second, first):
        return jnp.where(c == 0, second * NX + first, first * NX + second)

    def ppeer(d):
        return lax.rem(p + d, NX)

    def qpeer(d):
        return lax.rem(q + d, NX)

    def zpeer(d):
        return lax.rem(z + d, NZ)

    def pdev(d):
        return (natural(q, ppeer(d)) * 2 + c, z)

    def qdev(d):
        return (natural(qpeer(d), p) * 2 + c, z)

    def zdev(d):
        return (w, zpeer(d))

    barrier = pltpu.get_barrier_semaphore()
    peers = [sibling] + [pdev(d) for d in (1, 2, 3)] + [qdev(d) for d in (1, 2, 3)]
    peers += [zdev(d) for d in range(1, NZ)]
    for dev in peers:
        pl.semaphore_signal(barrier, inc=1, device_id=dev, device_id_type=MESH)

    sent = []
    drained = []

    def send(src, dst, ss, rs, dev):
        copy = pltpu.make_async_remote_copy(
            src_ref=src, dst_ref=dst, send_sem=ss, recv_sem=rs, device_id=dev, device_id_type=MESH
        )
        copy.start()
        sent.append(copy)
        return copy

    def drain(count):
        while len(drained) < count:
            copy = sent[len(drained)]
            copy.wait_send()
            drained.append(copy)

    k_rows = wo.shape[1]
    f_rows = wd.shape[1]
    d_cols = pl.ds(pl.multiple_of(c * units, 128), units)
    d_cols_sib = pl.ds(pl.multiple_of((1 - c) * units, 128), units)
    half = kv.shape[0] // STREAMS
    small = [
        pltpu.make_async_copy(src, dst, lsem.at[8 + i])
        for i, (src, dst) in enumerate((
            (q_hbm, q_ref), (nk_hbm, nk_ref), (nv_hbm, nv_ref), (res_hbm, res_ref),
            (gain_hbm, gain_ref),
        ))
    ]
    loads = []
    for s in range(STREAMS):
        rows = pl.ds(s * half, half)
        loads.append(pltpu.make_async_copy(k_hbm.at[rows], kv.at[rows], lsem.at[2 * s]))
        loads.append(pltpu.make_async_copy(v_hbm.at[rows], vv.at[rows], lsem.at[2 * s + 1]))
    own_rows = pl.ds(pl.multiple_of(c * k_rows, 128), k_rows)
    sib_rows = pl.ds(pl.multiple_of((1 - c) * k_rows, 128), k_rows)
    own_units = pl.ds(pl.multiple_of(c * f_rows, 128), f_rows)
    sib_units = pl.ds(pl.multiple_of((1 - c) * f_rows, 128), f_rows)
    load_wo = pltpu.make_async_copy(wo_hbm.at[own_rows], wo.at[0], lsem.at[4])
    load_wg = pltpu.make_async_copy(wg_hbm.at[:, d_cols], wg.at[0:depth], lsem.at[5])
    load_wu = pltpu.make_async_copy(wu_hbm.at[:, d_cols], wu.at[0:depth], lsem.at[6])
    load_wd = pltpu.make_async_copy(wd_hbm.at[own_units], wd.at[0], lsem.at[7])
    for copy in small + loads + [load_wo, load_wg, load_wu, load_wd]:
        copy.start()

    for copy in small:
        copy.wait()
    heads = q_ref.shape[1] // HD
    seqs = q_ref.shape[0]
    for h in range(heads):
        qs[pl.ds(h, seqs, stride=heads), :] = q_ref[:, h * HD:(h + 1) * HD].astype(F32)

    scale = 1.0 / math.sqrt(HD)

    def attend(s):
        loads[2 * s].wait()
        loads[2 * s + 1].wait()
        ctx = kv.shape[1]
        position = lax.broadcasted_iota(jnp.int32, (heads, ctx), 1)
        items = range(half)
        seq = [s * half + i for i in items]
        query = [qs[n * heads:(n + 1) * heads, :] for n in seq]
        score = [
            lax.dot_general(
                query[i].astype(BF16), kv[seq[i]], (((1,), (1,)), ((), ())),
                preferred_element_type=F32,
            )
            for i in items
        ]
        own = [
            jnp.sum(query[i] * nk_ref[n:n + 1, :].astype(F32), axis=1, keepdims=True) * scale
            for i, n in enumerate(seq)
        ]
        live = [position < len_ref[n] for n in seq]
        score = [jnp.where(live[i], score[i] * scale, -1e30) for i in items]
        top = [jnp.maximum(jnp.max(score[i], axis=1, keepdims=True), own[i]) for i in items]
        raw = [jnp.where(live[i], jnp.exp(score[i] - top[i]), 0.0) for i in items]
        own_raw = [jnp.exp(own[i] - top[i]) for i in items]
        inverse = [1.0 / (jnp.sum(raw[i], axis=1, keepdims=True) + own_raw[i]) for i in items]
        weights = [(raw[i] * inverse[i]).astype(BF16) for i in items]
        own_weight = [(own_raw[i] * inverse[i]).astype(BF16).astype(F32) for i in items]
        mixed = [jnp.dot(weights[i], vv[seq[i]], preferred_element_type=F32) for i in items]
        for i, n in enumerate(seq):
            ao[s, i * heads:(i + 1) * heads, :] = (
                mixed[i] + own_weight[i] * nv_ref[n:n + 1, :].astype(F32)
            )

    per_core = heads // 2

    def swap_start(s):
        for h in range(per_core):
            cols = slice(h * HD, (h + 1) * HD)
            ps[s, 0, :, cols] = ao[s, pl.ds(c * per_core + h, half, stride=heads), :]
            ps[s, 1, :, cols] = ao[s, pl.ds((1 - c) * per_core + h, half, stride=heads), :]
        return send(ps.at[s, 1], pr.at[s], d2s.at[s, 0], d2r.at[s, 0], sibling)

    def gather_first(s, k, buf):
        return [
            send(buf.at[s, q, p], buf.at[s, q, p], p4s.at[s, k, d - 1], p4r.at[s, k, d - 1], pdev(d))
            for d in (2, 1, 3)
        ]

    def gather_second(s, k, buf):
        return [
            send(buf.at[s, q], buf.at[s, q], p4s.at[s, k, d - 1], p4r.at[s, k, d - 1], qdev(d))
            for d in (2, 1, 3)
        ]

    def arrive(copies):
        for copy in copies:
            copy.wait_recv()

    def swap_end_gather(s, copy):
        copy.wait_recv()
        mine = ps[s, 0]
        theirs = pr[s]
        first = jnp.where(c == 0, mine, theirs)
        second = jnp.where(c == 0, theirs, mine)
        block = jnp.concatenate([first, second], axis=0).astype(BF16)
        ag[s, q, p] = block
        return gather_first(s, 0, ag)

    rows = NX * NY * 16

    def project(s, k, buf, weight, first=0, last=True):
        depth_here = buf.shape[-1]
        copy = None
        for half_index in (1, 0):
            for n in range(weight.shape[-1] // 256):
                cols = slice(n * 256, (n + 1) * 256)
                acc = jnp.dot(buf[s].reshape(rows, depth_here),
                              weight[half_index, first:first + depth_here, cols],
                              preferred_element_type=F32)
                for a in range(NY):
                    for b in range(NX):
                        r = (a * NX + b) * 16
                        to = pl.ds(pl.multiple_of(natural(a, b) * 16, 16), 16)
                        value = acc[r:r + 16]
                        held = psum if half_index else po.at[s, k]
                        if first:
                            value = value + held[to, cols]
                        if half_index and last:
                            cs[s, k, to, cols] = value.astype(BF16)
                        else:
                            held[to, cols] = value
            if half_index and last:
                copy = send(cs.at[s, k], cr.at[s, k], d2s.at[s, 1 + k], d2r.at[s, 1 + k], sibling)
        return copy

    share = rows // NZ
    top, bottom = slice(0, share // 2), slice(share // 2, share)

    def zsend(s, k, i, src, dst, d):
        return send(src, dst, zss.at[s, k, i], zrs.at[s, k, i], zdev(d))

    def scatter_z(s, k, copy):
        copy.wait_recv()
        for j in range(NZ):
            r = slice(j * share, (j + 1) * share)
            zs[s, k, j] = (po[s, k, r, :] + cr[s, k, r, :].astype(F32)).astype(BF16)
        src = [zs.at[s, k, zpeer(d)] for d in range(NZ)]
        return [
            zsend(s, k, 0, src[4].at[top], zr.at[s, k, 0, top], 2),
            zsend(s, k, 1, src[4].at[bottom], zr.at[s, k, 1, bottom], 6),
            zsend(s, k, 2, src[3], zr.at[s, k, 2], 1),
            zsend(s, k, 3, src[5], zr.at[s, k, 3], 7),
            zsend(s, k, 4, src[1], zr.at[s, k, 4], 1),
            zsend(s, k, 5, src[7], zr.at[s, k, 5], 7),
        ]

    def relay_z(s, k, copies):
        for i, (part, d) in enumerate(((top, 2), (bottom, 6))):
            copies[i].wait_recv()
            copies[2 + i].wait_recv()
            to = zpeer(d)
            zt[s, k, i] = (zs[s, k, to].astype(F32) + zr[s, k, 2 + i].astype(F32)).astype(BF16)
            zt[s, k, i, part] = (
                zs[s, k, to, part].astype(F32) + zr[s, k, 2 + i, part].astype(F32)
                + zr[s, k, i, part].astype(F32)
            ).astype(BF16)
            copies.append(zsend(s, k, 6 + i, zt.at[s, k, i], zr.at[s, k, 6 + i], d))
        return copies[4:]

    def sum_z(s, k, copies):
        own = pl.ds(pl.multiple_of(z * share, share), share)
        acc = po[s, k, own, :] + cr[s, k, own, :].astype(F32)
        arrive(copies)
        for i in range(4, 8):
            acc += zr[s, k, i].astype(F32)
        return acc

    def norm_gather(s, copies):
        stream = sum_z(s, 0, copies)
        pieces = [
            res_ref[g * 16:(g + 1) * 16, :].astype(F32)[s * 8:(s + 1) * 8] for g in range(share // 8)
        ]
        stream = stream + jnp.concatenate(pieces, axis=0)
        st[s] = stream
        xn[s, z, :, 0:depth] = (stream * gain_ref[...]).astype(BF16)
        block = xn.at[s, z, :, 0:depth]
        return [zsend(s, 2, i, block, block, d) for i, d in enumerate((2, 6, 1, 7))]

    def relay_normed(s, copies):
        for i, (part, near, far) in enumerate(((top, 1, 2), (bottom, 7, 6))):
            copies[i].wait_recv()
            came = zpeer(NZ - far)
            half_block = xn.at[s, came, part, 0:depth]
            block = xn.at[s, came, :, 0:depth]
            copies.append(zsend(s, 2, 4 + 2 * i, half_block, half_block, far))
            copies.append(zsend(s, 2, 5 + 2 * i, block, block, near))
        return copies[2:]

    def encode(value):
        high = value.astype(BF16).astype(F32)
        lane = lax.broadcasted_iota(jnp.int32, value.shape, 1)
        return jnp.where(lane < 64, high, value - high).astype(BF16)

    def decode(pair):
        value = pair.astype(F32)
        return value + pltpu.roll(value, 64, 1)

    def row_squares(s, first):
        gain = gain_sib if first else gain_ref
        ungain = 1.0 / gain[...]
        for j in range(NZ):
            value = xn[s, j, :, first:first + depth].astype(F32) * ungain
            value = value * value
            total = value[:, 0:128]
            for n in range(1, depth // 128):
                total += value[:, n * 128:(n + 1) * 128]
            r = slice(j * share, (j + 1) * share)
            if first:
                total += sq[r, :]
                total = jnp.broadcast_to(jnp.sum(total, axis=1, keepdims=True), (share, 128))
            sq[r, :] = total

    def swap_normed(s, copies):
        arrive(copies)
        return send(xn.at[s, :, :, 0:depth], xn.at[s, :, :, depth:2 * depth],
                    d2s.at[s, 3], d2r.at[s, 3], sibling)

    parts = [(0, ac[0].shape[-1]), (ac[0].shape[-1], ac[1].shape[-1])]

    def spread(buf, s, cols, value):
        for j in range(NY):
            for i in range(NX):
                r = (j * NX + i) * 16
                first = jnp.where(c == 0, i, j)
                second = jnp.where(c == 0, j, i)
                buf[s, first, second, :, cols] = value[r:r + 16]

    def expand(s, part):
        base, count = parts[part]
        for weight, buf in ((wg, ga[part]), (wu, gb[part])):
            for start in range(0, count, 256):
                size = min(256, count - start)
                acc = jnp.dot(xn[s].reshape(rows, 2 * depth),
                              weight[:, base + start:base + start + size],
                              preferred_element_type=F32)
                spread(buf, s, slice(start, start + size), acc.astype(BF16))

    def plane_send(s, part, i, src, dst, d):
        return send(src, dst, p4s.at[s, 2 + part, i], p4r.at[s, 2 + part, i], pdev(d))

    def scatter_first(s, part):
        a, b, ta, tb = ga[part], gb[part], ra[part], rb[part]
        return [
            plane_send(s, part, 0, a.at[s, ppeer(2)], ta.at[s, 0], 1),
            plane_send(s, part, 1, b.at[s, ppeer(2)], tb.at[s, 0], 3),
            plane_send(s, part, 2, a.at[s, ppeer(3)], ta.at[s, 1], 3),
            plane_send(s, part, 3, b.at[s, ppeer(1)], tb.at[s, 1], 1),
        ]

    def add_rows(terms, count, out, base, squares_too):
        def block(j, _):
            blocks = [get(j) for get in terms]
            acc = blocks[0][:, 0:count].astype(F32)
            for value in blocks[1:]:
                acc += value[:, 0:count].astype(F32)
            out[j, :, base:base + count] = acc.astype(BF16)
            if squares_too:
                square = decode(blocks[0][:, count:])
                for value in blocks[1:]:
                    square += decode(value[:, count:])
                end = out.shape[-1]
                out[j, :, end - 128:end] = encode(square)
            return 0
        lax.fori_loop(0, NY, block, 0)

    def relay(s, part, copies):
        a, b, ta, tb = ga[part], gb[part], ra[part], rb[part]
        count = parts[part][1]
        copies[0].wait_recv()
        add_rows([lambda j: a[s, ppeer(1), j], lambda j: ta[s, 0, j]], count,
                 ha[part].at[s], 0, part == 0)
        copies.append(plane_send(s, part, 4, ha[part].at[s], ta.at[s, 2], 1))
        copies[1].wait_recv()
        add_rows([lambda j: b[s, ppeer(3), j], lambda j: tb[s, 0, j]], count,
                 hb[part].at[s], 0, False)
        copies.append(plane_send(s, part, 5, hb[part].at[s], tb.at[s, 2], 3))
        return copies[2:]

    def scatter_second(s, part, copies):
        a, b, ta, tb = ga[part], gb[part], ra[part], rb[part]
        count = parts[part][1]
        arrive(copies)
        add_rows([lambda j: a[s, p, j], lambda j: ta[s, 1, j], lambda j: ta[s, 2, j]], count,
                 gp[part].at[s], 0, part == 0)
        add_rows([lambda j: b[s, p, j], lambda j: tb[s, 1, j], lambda j: tb[s, 2, j]], count,
                 gp[part].at[s], count, False)
        return [
            send(gp[part].at[s, qpeer(d)], gr2[part].at[s, d - 1],
                 p4s.at[s, 4 + part, d - 1], p4r.at[s, 4 + part, d - 1], qdev(d))
            for d in (2, 1, 3)
        ]

    def activate(s, part, copies):
        arrive(copies)
        count = parts[part][1]
        if part == 0:
            square = decode(gp[0][s, q, :, 2 * count:])
            for d in range(3):
                square += decode(gr2[0][s, d, :, 2 * count:])
            scales[s] = lax.rsqrt(square / D + EPS)
        factor = scales[s]
        for n in range(count // 128):
            cols = slice(n * 128, (n + 1) * 128)
            lift_cols = slice(count + n * 128, count + (n + 1) * 128)
            gate = gp[part][s, q, :, cols].astype(F32)
            lift = gp[part][s, q, :, lift_cols].astype(F32)
            for d in range(3):
                gate += gr2[part][s, d, :, cols].astype(F32)
                lift += gr2[part][s, d, :, lift_cols].astype(F32)
            gate = gate * factor
            ac[part][s, q, p, :, cols] = (
                gate / (1.0 + jnp.exp(-gate)) * (lift * factor)
            ).astype(BF16)
        return gather_first(s, 6 + part, ac[part])

    def gather_on(s, part, copies):
        arrive(copies)
        return gather_second(s, 8 + part, ac[part])

    def down(s, part, copies):
        arrive(copies)
        return project(s, 1, ac[part], wd, parts[part][0], part == 1)

    def squares(s, copy):
        row_squares(s, 0)
        copy.wait_recv()
        row_squares(s, depth)
        count = parts[0][1]
        spread(ga[0], s, slice(count, count + 128), encode(sq[...]))

    S = range(STREAMS)
    for s in S:
        attend(s)
    pl.semaphore_wait(barrier, len(peers))
    swaps = [swap_start(s) for s in S]
    share_gain = send(gain_hbm, gain_sib, wss.at[4], wrs.at[4], sibling)
    share_wo = send(wo_hbm.at[sib_rows], wo.at[1], wss.at[0], wrs.at[0], sibling)
    a1 = [swap_end_gather(s, swaps[s]) for s in S]
    share_wg = send(wg_hbm.at[:, d_cols_sib], wg.at[depth:2 * depth], wss.at[1], wrs.at[1], sibling)
    share_wu = send(wu_hbm.at[:, d_cols_sib], wu.at[depth:2 * depth], wss.at[2], wrs.at[2], sibling)
    a2 = []
    for s in S:
        arrive(a1[s])
        a2.append(gather_second(s, 1, ag))
    load_wo.wait()
    share_wo.wait_recv()
    r1 = []
    for s in S:
        arrive(a2[s])
        c1 = project(s, 0, ag, wo)
        r1.append(scatter_z(s, 0, c1))
    share_wd = send(wd_hbm.at[sib_units], wd.at[1], wss.at[3], wrs.at[3], sibling)
    for copy in (load_wg, load_wu, load_wd):
        copy.wait()
    for copy in (share_gain, share_wg, share_wu):
        copy.wait_recv()
    drain(16)
    r1 = [relay_z(s, 0, r1[s]) for s in S]
    n1 = [norm_gather(s, r1[s]) for s in S]
    n1 = [relay_normed(s, n1[s]) for s in S]
    drain(32)
    share_wd.wait_recv()
    squares(0, swap_normed(0, n1[0]))
    expand(0, 0)
    e1 = {(0, 0): scatter_first(0, 0)}
    expand(0, 1)
    e1[0, 1] = scatter_first(0, 1)
    squares(1, swap_normed(1, n1[1]))
    drain(40)
    e2, f1, f2 = {}, {}, {}
    e1[0, 0] = relay(0, 0, e1[0, 0])
    expand(1, 0)
    e1[0, 1] = relay(0, 1, e1[0, 1])
    e1[1, 0] = scatter_first(1, 0)
    expand(1, 1)
    e2[0, 0] = scatter_second(0, 0, e1[0, 0])
    e1[1, 1] = scatter_first(1, 1)
    e2[0, 1] = scatter_second(0, 1, e1[0, 1])
    e1[1, 0] = relay(1, 0, e1[1, 0])
    f1[0, 0] = activate(0, 0, e2[0, 0])
    e1[1, 1] = relay(1, 1, e1[1, 1])
    f1[0, 1] = activate(0, 1, e2[0, 1])
    e2[1, 0] = scatter_second(1, 0, e1[1, 0])
    f2[0, 0] = gather_on(0, 0, f1[0, 0])
    e2[1, 1] = scatter_second(1, 1, e1[1, 1])
    f2[0, 1] = gather_on(0, 1, f1[0, 1])
    f1[1, 0] = activate(1, 0, e2[1, 0])
    f1[1, 1] = activate(1, 1, e2[1, 1])
    down(0, 0, f2[0, 0])
    f2[1, 0] = gather_on(1, 0, f1[1, 0])
    f2[1, 1] = gather_on(1, 1, f1[1, 1])
    c2 = down(0, 1, f2[0, 1])
    r2 = [scatter_z(0, 1, c2)]
    drain(len(sent) - 30)
    down(1, 0, f2[1, 0])
    r2[0] = relay_z(0, 1, r2[0])
    c2 = down(1, 1, f2[1, 1])
    r2.append(scatter_z(1, 1, c2))
    drain(len(sent) - 16)
    r2[1] = relay_z(1, 1, r2[1])
    for s in S:
        fin[s] = st[s] + sum_z(s, 1, r2[s])
    for g in range(share // 8):
        out_ref[g * 16:(g + 1) * 16, :] = jnp.concatenate(
            [fin[s, g * 8:(g + 1) * 8, :] for s in S], axis=0
        ).astype(BF16)
    drain(len(sent))


def local(
    queries, cache_keys, cache_values, new_key, new_value, lengths,
    out_weight, residual, norm_gain, gate_weight, up_weight, down_weight,
):
    seqs, ctx, _ = cache_keys.shape
    heads = queries.shape[1] // HD
    half = seqs // STREAMS
    kh = out_weight.shape[0] // 2
    cols = out_weight.shape[1]
    depth, hidden = gate_weight.shape
    units = hidden // 2
    cut = units // 256 * 128
    w0, w1 = 2 * cut + 128, 2 * (units - cut)
    rows = NX * NY * 2 * half
    share = rows // NZ
    S = STREAMS
    DMA = pltpu.SemaphoreType.DMA

    def v(*shape, dtype=BF16):
        return pltpu.VMEM(shape, dtype)

    scratch = [
        v(*queries.shape), v(*new_key.shape), v(*new_value.shape), v(*residual.shape),
        v(1, cols, dtype=F32),
        v(seqs, ctx, HD), v(seqs, ctx, HD),
        v(2, kh, cols), v(2 * depth, units), v(2 * depth, units), v(2, units, cols),
        v(1, cols, dtype=F32),
        v(seqs * heads, HD, dtype=F32),
        v(S, half * heads, HD, dtype=F32),
        v(S, 2, half, kh, dtype=F32), v(S, half, kh, dtype=F32),
        v(S, NY, NX, 16, kh),
        v(S, 2, rows, cols, dtype=F32),
        v(S, 2, rows, cols), v(S, 2, rows, cols),
        v(S, 2, NZ, share, cols), v(S, 2, 8, share, cols),
        v(S, 2, 2, share, cols),
        v(S, share, cols, dtype=F32),
        v(S, NZ, share, 2 * depth), v(rows, 128, dtype=F32),
        v(S, NX, NY, 16, cut + 128), v(S, NX, NY, 16, units - cut),
        v(S, NX, NY, 16, cut), v(S, NX, NY, 16, units - cut),
        v(S, 3, NY, 16, cut + 128), v(S, 3, NY, 16, units - cut),
        v(S, 3, NY, 16, cut), v(S, 3, NY, 16, units - cut),
        v(S, NY, 16, cut + 128), v(S, NY, 16, units - cut),
        v(S, NY, 16, cut), v(S, NY, 16, units - cut),
        v(S, NY, 16, w0), v(S, NY, 16, w1),
        v(S, 3, 16, w0), v(S, 3, 16, w1),
        v(S, NY, NX, 16, cut), v(S, NY, NX, 16, units - cut),
        v(rows, cols, dtype=F32), v(S, 16, 128, dtype=F32),
        v(S, share, cols, dtype=F32),
        DMA((13,)), DMA((5,)), DMA((5,)),
        DMA((S, 4)), DMA((S, 4)),
        DMA((S, 10, 6)), DMA((S, 10, 6)),
        DMA((S, 3, 8)), DMA((S, 3, 8)),
    ]
    vm = pl.BlockSpec(memory_space=pltpu.VMEM)
    hbm = pl.BlockSpec(memory_space=pl.ANY)
    return pl.pallas_call(
        body,
        out_shape=jax.ShapeDtypeStruct(residual.shape, BF16),
        in_specs=[pl.BlockSpec(memory_space=pltpu.SMEM)] + [hbm] * 11,
        out_specs=vm,
        scratch_shapes=scratch,
        compiler_params=pltpu.CompilerParams(
            collective_id=0, has_side_effects=True, vmem_limit_bytes=58 << 20
        ),
        name="layer",
    )(
        lengths, queries, new_key, new_value, residual, norm_gain.reshape(1, -1),
        cache_keys, cache_values, out_weight, gate_weight, up_weight, down_weight,
    )


def solution(mesh):
    in_specs = (
        P("wide", "narrow"),
        P("wide", None, "narrow"),
        P("wide", None, "narrow"),
        P("wide", "narrow"),
        P("wide", "narrow"),
        P("wide"),
        P("narrow", "wide"),
        P("narrow", "wide"),
        P("wide"),
        P("wide", "narrow"),
        P("wide", "narrow"),
        P("narrow", "wide"),
    )
    out_specs = P("narrow", "wide")
    return jax.shard_map(local, mesh=mesh, in_specs=in_specs, out_specs=out_specs, check_vma=False)
```

```python
import functools
import math

import jax
import jax.numpy as jnp
from jax import lax
from jax.experimental import pallas as pl
from jax.experimental.pallas import tpu as pltpu
from jax.sharding import PartitionSpec as P

D = 16384
HD = 128
EPS = 1e-05
NX, NY, NZ = 4, 4, 8
STREAMS = 2
MESH = pl.DeviceIdType.MESH
F32 = jnp.float32
BF16 = jnp.bfloat16


def body(
    len_ref, q_hbm, nk_hbm, nv_hbm, res_hbm, gain_hbm,
    k_hbm, v_hbm, wo_hbm, wg_hbm, wu_hbm, wd_hbm,
    out_ref,
    q_ref, nk_ref, nv_ref, res_ref, gain_ref, kv, vv, wo, wg, wu, wd, gain_sib, qs, ao, ps, pr, ag, po, cs, cr, zs, zr, zt, st,
    xn, sq, ga0, ga1, gb0, gb1, ra0, ra1, rb0, rb1, ha0, ha1, hb0, hb1, gp0, gp1, gr20, gr21, ac0, ac1, psum, scales, fin,
    lsem, wss, wrs, d2s, d2r, p4s, p4r, zss, zrs,
):
    ga, gb, ra, rb = (ga0, ga1), (gb0, gb1), (ra0, ra1), (rb0, rb1)
    ha, hb, gp, gr2, ac = (ha0, ha1), (hb0, hb1), (gp0, gp1), (gr20, gr21), (ac0, ac1)
    w = lax.axis_index("wide")
    z = lax.axis_index("narrow")
    c = lax.rem(w, 2)
    chip = lax.div(w, 2)
    x = lax.rem(chip, NX)
    y = lax.div(chip, NX)
    units = wg.shape[1]
    depth = wg.shape[0] // 2

    sibling = (chip * 2 + (1 - c), z)

    p = jnp.where(c == 0, x, y)
    q = jnp.where(c == 0, y, x)

    def natural(second, first):
        return jnp.where(c == 0, second * NX + first, first * NX + second)

    def ppeer(d):
        return lax.rem(p + d, NX)

    def qpeer(d):
        return lax.rem(q + d, NX)

    def zpeer(d):
        return lax.rem(z + d, NZ)

    def pdev(d):
        return (natural(q, ppeer(d)) * 2 + c, z)

    def qdev(d):
        return (natural(qpeer(d), p) * 2 + c, z)

    def zdev(d):
        return (w, zpeer(d))

    barrier = pltpu.get_barrier_semaphore()
    peers = [sibling] + [pdev(d) for d in (1, 2, 3)] + [qdev(d) for d in (1, 2, 3)]
    peers += [zdev(d) for d in range(1, NZ)]
    for dev in peers:
        pl.semaphore_signal(barrier, inc=1, device_id=dev, device_id_type=MESH)

    sent = []
    drained = []

    def send(src, dst, ss, rs, dev):
        copy = pltpu.make_async_remote_copy(
            src_ref=src, dst_ref=dst, send_sem=ss, recv_sem=rs, device_id=dev, device_id_type=MESH
        )
        copy.start()
        sent.append(copy)
        return copy

    def drain(count):
        while len(drained) < count:
            copy = sent[len(drained)]
            copy.wait_send()
            drained.append(copy)

    k_rows = wo.shape[1]
    f_rows = wd.shape[1]
    d_cols = pl.ds(pl.multiple_of(c * units, 128), units)
    d_cols_sib = pl.ds(pl.multiple_of((1 - c) * units, 128), units)
    half = kv.shape[0] // STREAMS
    small = [
        pltpu.make_async_copy(src, dst, lsem.at[8 + i])
        for i, (src, dst) in enumerate((
            (q_hbm, q_ref), (nk_hbm, nk_ref), (nv_hbm, nv_ref), (res_hbm, res_ref),
            (gain_hbm, gain_ref),
        ))
    ]
    loads = []
    for s in range(STREAMS):
        rows = pl.ds(s * half, half)
        loads.append(pltpu.make_async_copy(k_hbm.at[rows], kv.at[rows], lsem.at[2 * s]))
        loads.append(pltpu.make_async_copy(v_hbm.at[rows], vv.at[rows], lsem.at[2 * s + 1]))
    own_rows = pl.ds(pl.multiple_of(c * k_rows, 128), k_rows)
    sib_rows = pl.ds(pl.multiple_of((1 - c) * k_rows, 128), k_rows)
    own_units = pl.ds(pl.multiple_of(c * f_rows, 128), f_rows)
    sib_units = pl.ds(pl.multiple_of((1 - c) * f_rows, 128), f_rows)
    load_wo = pltpu.make_async_copy(wo_hbm.at[own_rows], wo.at[0], lsem.at[4])
    load_wg = pltpu.make_async_copy(wg_hbm.at[:, d_cols], wg.at[0:depth], lsem.at[5])
    load_wu = pltpu.make_async_copy(wu_hbm.at[:, d_cols], wu.at[0:depth], lsem.at[6])
    load_wd = pltpu.make_async_copy(wd_hbm.at[own_units], wd.at[0], lsem.at[7])
    for copy in small + loads + [load_wo, load_wg, load_wu, load_wd]:
        copy.start()

    for copy in small:
        copy.wait()
    heads = q_ref.shape[1] // HD
    seqs = q_ref.shape[0]
    for h in range(heads):
        qs[pl.ds(h, seqs, stride=heads), :] = q_ref[:, h * HD:(h + 1) * HD].astype(F32)

    scale = 1.0 / math.sqrt(HD)

    def attend(s):
        loads[2 * s].wait()
        loads[2 * s + 1].wait()
        ctx = kv.shape[1]
        position = lax.broadcasted_iota(jnp.int32, (heads, ctx), 1)
        items = range(half)
        seq = [s * half + i for i in items]
        query = [qs[n * heads:(n + 1) * heads, :] for n in seq]
        score = [
            lax.dot_general(
                query[i].astype(BF16), kv[seq[i]], (((1,), (1,)), ((), ())),
                preferred_element_type=F32,
            )
            for i in items
        ]
        own = [
            jnp.sum(query[i] * nk_ref[n:n + 1, :].astype(F32), axis=1, keepdims=True) * scale
            for i, n in enumerate(seq)
        ]
        live = [position < len_ref[n] for n in seq]
        score = [jnp.where(live[i], score[i] * scale, -1e30) for i in items]
        top = [jnp.maximum(jnp.max(score[i], axis=1, keepdims=True), own[i]) for i in items]
        raw = [jnp.where(live[i], jnp.exp(score[i] - top[i]), 0.0) for i in items]
        own_raw = [jnp.exp(own[i] - top[i]) for i in items]
        inverse = [1.0 / (jnp.sum(raw[i], axis=1, keepdims=True) + own_raw[i]) for i in items]
        weights = [(raw[i] * inverse[i]).astype(BF16) for i in items]
        own_weight = [(own_raw[i] * inverse[i]).astype(BF16).astype(F32) for i in items]
        mixed = [jnp.dot(weights[i], vv[seq[i]], preferred_element_type=F32) for i in items]
        for i, n in enumerate(seq):
            ao[s, i * heads:(i + 1) * heads, :] = (
                mixed[i] + own_weight[i] * nv_ref[n:n + 1, :].astype(F32)
            )

    per_core = heads // 2

    def swap_start(s):
        for h in range(per_core):
            cols = slice(h * HD, (h + 1) * HD)
            ps[s, 0, :, cols] = ao[s, pl.ds(c * per_core + h, half, stride=heads), :]
            ps[s, 1, :, cols] = ao[s, pl.ds((1 - c) * per_core + h, half, stride=heads), :]
        return send(ps.at[s, 1], pr.at[s], d2s.at[s, 0], d2r.at[s, 0], sibling)

    def gather_first(s, k, buf):
        return [
            send(buf.at[s, q, p], buf.at[s, q, p], p4s.at[s, k, d - 1], p4r.at[s, k, d - 1], pdev(d))
            for d in (2, 1, 3)
        ]

    def gather_second(s, k, buf):
        return [
            send(buf.at[s, q], buf.at[s, q], p4s.at[s, k, d - 1], p4r.at[s, k, d - 1], qdev(d))
            for d in (2, 1, 3)
        ]

    low, high = slice(0, NX // 2), slice(NX // 2, NX)

    def gather_around(s, k, buf):
        return [
            send(buf.at[s, q, part], buf.at[s, q, part], p4s.at[s, k, i], p4r.at[s, k, i], qdev(d))
            for i, (part, d) in enumerate(((low, 1), (high, 3), (high, 1), (low, 3)))
        ]

    def forward(s, k, buf, copies):
        for i, (part, d) in enumerate(((low, 1), (high, 3))):
            copies[i].wait_recv()
            block = buf.at[s, qpeer(4 - d), part]
            copies.append(send(block, block, p4s.at[s, k, 4 + i], p4r.at[s, k, 4 + i], qdev(d)))
        return copies[2:]

    def arrive(copies):
        for copy in copies:
            copy.wait_recv()

    def swap_end_gather(s, copy):
        copy.wait_recv()
        mine = ps[s, 0]
        theirs = pr[s]
        first = jnp.where(c == 0, mine, theirs)
        second = jnp.where(c == 0, theirs, mine)
        block = jnp.concatenate([first, second], axis=0).astype(BF16)
        ag[s, q, p] = block
        return gather_first(s, 0, ag)

    rows = NX * NY * 16

    def project(s, k, buf, weight, first=0, last=True):
        depth_here = buf.shape[-1]
        copy = None
        for half_index in (1, 0):
            for n in range(weight.shape[-1] // 256):
                cols = slice(n * 256, (n + 1) * 256)
                acc = jnp.dot(buf[s].reshape(rows, depth_here),
                              weight[half_index, first:first + depth_here, cols],
                              preferred_element_type=F32)
                for a in range(NY):
                    for b in range(NX):
                        r = (a * NX + b) * 16
                        to = pl.ds(pl.multiple_of(natural(a, b) * 16, 16), 16)
                        value = acc[r:r + 16]
                        held = psum if half_index else po.at[s, k]
                        if first:
                            value = value + held[to, cols]
                        if half_index and last:
                            cs[s, k, to, cols] = value.astype(BF16)
                        else:
                            held[to, cols] = value
            if half_index and last:
                copy = send(cs.at[s, k], cr.at[s, k], d2s.at[s, 1 + k], d2r.at[s, 1 + k], sibling)
        return copy

    share = rows // NZ
    top, bottom = slice(0, share // 2), slice(share // 2, share)

    def zsend(s, k, i, src, dst, d):
        return send(src, dst, zss.at[s, k, i], zrs.at[s, k, i], zdev(d))

    def scatter_z(s, k, copy):
        copy.wait_recv()
        for j in range(NZ):
            r = slice(j * share, (j + 1) * share)
            zs[s, k, j] = (po[s, k, r, :] + cr[s, k, r, :].astype(F32)).astype(BF16)
        src = [zs.at[s, k, zpeer(d)] for d in range(NZ)]
        return [
            zsend(s, k, 0, src[4].at[top], zr.at[s, k, 0, top], 2),
            zsend(s, k, 1, src[4].at[bottom], zr.at[s, k, 1, bottom], 6),
            zsend(s, k, 2, src[3], zr.at[s, k, 2], 1),
            zsend(s, k, 3, src[5], zr.at[s, k, 3], 7),
            zsend(s, k, 4, src[1], zr.at[s, k, 4], 1),
            zsend(s, k, 5, src[7], zr.at[s, k, 5], 7),
        ]

    def relay_z(s, k, copies):
        for i, (part, d) in enumerate(((top, 2), (bottom, 6))):
            copies[i].wait_recv()
            copies[2 + i].wait_recv()
            to = zpeer(d)
            zt[s, k, i] = (zs[s, k, to].astype(F32) + zr[s, k, 2 + i].astype(F32)).astype(BF16)
            zt[s, k, i, part] = (
                zs[s, k, to, part].astype(F32) + zr[s, k, 2 + i, part].astype(F32)
                + zr[s, k, i, part].astype(F32)
            ).astype(BF16)
            copies.append(zsend(s, k, 6 + i, zt.at[s, k, i], zr.at[s, k, 6 + i], d))
        return copies[4:]

    def sum_z(s, k, copies):
        own = pl.ds(pl.multiple_of(z * share, share), share)
        acc = po[s, k, own, :] + cr[s, k, own, :].astype(F32)
        arrive(copies)
        for i in range(4, 8):
            acc += zr[s, k, i].astype(F32)
        return acc

    def norm_gather(s, copies):
        stream = sum_z(s, 0, copies)
        pieces = [
            res_ref[g * 16:(g + 1) * 16, :].astype(F32)[s * 8:(s + 1) * 8] for g in range(share // 8)
        ]
        stream = stream + jnp.concatenate(pieces, axis=0)
        st[s] = stream
        xn[s, z, :, 0:depth] = (stream * gain_ref[...]).astype(BF16)
        block = xn.at[s, z, :, 0:depth]
        return [zsend(s, 2, i, block, block, d) for i, d in enumerate((2, 6, 1, 7))]

    def relay_normed(s, copies):
        for i, (part, near, far) in enumerate(((top, 1, 2), (bottom, 7, 6))):
            copies[i].wait_recv()
            came = zpeer(NZ - far)
            half_block = xn.at[s, came, part, 0:depth]
            block = xn.at[s, came, :, 0:depth]
            copies.append(zsend(s, 2, 4 + 2 * i, half_block, half_block, far))
            copies.append(zsend(s, 2, 5 + 2 * i, block, block, near))
        return copies[2:]

    def encode(value):
        high = value.astype(BF16).astype(F32)
        lane = lax.broadcasted_iota(jnp.int32, value.shape, 1)
        return jnp.where(lane < 64, high, value - high).astype(BF16)

    def decode(pair):
        value = pair.astype(F32)
        return value + pltpu.roll(value, 64, 1)

    def row_squares(s, first):
        gain = gain_sib if first else gain_ref
        ungain = 1.0 / gain[...]
        for j in range(NZ):
            value = xn[s, j, :, first:first + depth].astype(F32) * ungain
            value = value * value
            total = value[:, 0:128]
            for n in range(1, depth // 128):
                total += value[:, n * 128:(n + 1) * 128]
            r = slice(j * share, (j + 1) * share)
            if first:
                total += sq[r, :]
                total = jnp.broadcast_to(jnp.sum(total, axis=1, keepdims=True), (share, 128))
            sq[r, :] = total

    def swap_normed(s, copies):
        arrive(copies)
        return send(xn.at[s, :, :, 0:depth], xn.at[s, :, :, depth:2 * depth],
                    d2s.at[s, 3], d2r.at[s, 3], sibling)

    parts = [(0, ac[0].shape[-1]), (ac[0].shape[-1], ac[1].shape[-1])]

    def spread(buf, s, cols, value):
        for j in range(NY):
            for i in range(NX):
                r = (j * NX + i) * 16
                first = jnp.where(c == 0, i, j)
                second = jnp.where(c == 0, j, i)
                buf[s, first, second, :, cols] = value[r:r + 16]

    def expand(s, part):
        base, count = parts[part]
        for weight, buf in ((wg, ga[part]), (wu, gb[part])):
            for start in range(0, count, 256):
                size = min(256, count - start)
                acc = jnp.dot(xn[s].reshape(rows, 2 * depth),
                              weight[:, base + start:base + start + size],
                              preferred_element_type=F32)
                spread(buf, s, slice(start, start + size), acc.astype(BF16))

    def plane_send(s, part, i, src, dst, d):
        return send(src, dst, p4s.at[s, 2 + part, i], p4r.at[s, 2 + part, i], pdev(d))

    def scatter_first(s, part):
        a, b, ta, tb = ga[part], gb[part], ra[part], rb[part]
        return [
            plane_send(s, part, 0, a.at[s, ppeer(2)], ta.at[s, 0], 1),
            plane_send(s, part, 1, b.at[s, ppeer(2)], tb.at[s, 0], 3),
            plane_send(s, part, 2, a.at[s, ppeer(3)], ta.at[s, 1], 3),
            plane_send(s, part, 3, b.at[s, ppeer(1)], tb.at[s, 1], 1),
        ]

    def add_rows(terms, count, out, base, squares_too):
        def block(j, _):
            blocks = [get(j) for get in terms]
            acc = blocks[0][:, 0:count].astype(F32)
            for value in blocks[1:]:
                acc += value[:, 0:count].astype(F32)
            out[j, :, base:base + count] = acc.astype(BF16)
            if squares_too:
                square = decode(blocks[0][:, count:])
                for value in blocks[1:]:
                    square += decode(value[:, count:])
                end = out.shape[-1]
                out[j, :, end - 128:end] = encode(square)
            return 0
        lax.fori_loop(0, NY, block, 0)

    def relay(s, part, copies):
        a, b, ta, tb = ga[part], gb[part], ra[part], rb[part]
        count = parts[part][1]
        copies[0].wait_recv()
        add_rows([lambda j: a[s, ppeer(1), j], lambda j: ta[s, 0, j]], count,
                 ha[part].at[s], 0, part == 0)
        copies.append(plane_send(s, part, 4, ha[part].at[s], ta.at[s, 2], 1))
        copies[1].wait_recv()
        add_rows([lambda j: b[s, ppeer(3), j], lambda j: tb[s, 0, j]], count,
                 hb[part].at[s], 0, False)
        copies.append(plane_send(s, part, 5, hb[part].at[s], tb.at[s, 2], 3))
        return copies[2:]

    def scatter_second(s, part, copies):
        a, b, ta, tb = ga[part], gb[part], ra[part], rb[part]
        count = parts[part][1]
        arrive(copies)
        add_rows([lambda j: a[s, p, j], lambda j: ta[s, 1, j], lambda j: ta[s, 2, j]], count,
                 gp[part].at[s], 0, part == 0)
        add_rows([lambda j: b[s, p, j], lambda j: tb[s, 1, j], lambda j: tb[s, 2, j]], count,
                 gp[part].at[s], count, False)
        return [
            send(gp[part].at[s, qpeer(d)], gr2[part].at[s, d - 1],
                 p4s.at[s, 4 + part, d - 1], p4r.at[s, 4 + part, d - 1], qdev(d))
            for d in (2, 1, 3)
        ]

    def activate(s, part, copies):
        arrive(copies)
        count = parts[part][1]
        if part == 0:
            square = decode(gp[0][s, q, :, 2 * count:])
            for d in range(3):
                square += decode(gr2[0][s, d, :, 2 * count:])
            scales[s] = lax.rsqrt(square / D + EPS)
        factor = scales[s]
        for n in range(count // 128):
            cols = slice(n * 128, (n + 1) * 128)
            lift_cols = slice(count + n * 128, count + (n + 1) * 128)
            gate = gp[part][s, q, :, cols].astype(F32)
            lift = gp[part][s, q, :, lift_cols].astype(F32)
            for d in range(3):
                gate += gr2[part][s, d, :, cols].astype(F32)
                lift += gr2[part][s, d, :, lift_cols].astype(F32)
            gate = gate * factor
            ac[part][s, q, p, :, cols] = (
                gate / (1.0 + jnp.exp(-gate)) * (lift * factor)
            ).astype(BF16)
        return gather_first(s, 6 + part, ac[part])

    def gather_on(s, part, copies):
        arrive(copies)
        return gather_around(s, 8 + part, ac[part])

    def down(s, part, copies):
        arrive(copies)
        return project(s, 1, ac[part], wd, parts[part][0], part == 1)

    def squares(s, copy):
        row_squares(s, 0)
        copy.wait_recv()
        row_squares(s, depth)
        count = parts[0][1]
        spread(ga[0], s, slice(count, count + 128), encode(sq[...]))

    S = range(STREAMS)
    for s in S:
        attend(s)
    pl.semaphore_wait(barrier, len(peers))
    swaps = [swap_start(s) for s in S]
    share_gain = send(gain_hbm, gain_sib, wss.at[4], wrs.at[4], sibling)
    share_wo = send(wo_hbm.at[sib_rows], wo.at[1], wss.at[0], wrs.at[0], sibling)
    a1 = [swap_end_gather(s, swaps[s]) for s in S]
    share_wg = send(wg_hbm.at[:, d_cols_sib], wg.at[depth:2 * depth], wss.at[1], wrs.at[1], sibling)
    share_wu = send(wu_hbm.at[:, d_cols_sib], wu.at[depth:2 * depth], wss.at[2], wrs.at[2], sibling)
    a2 = []
    for s in S:
        arrive(a1[s])
        a2.append(gather_second(s, 1, ag))
    load_wo.wait()
    share_wo.wait_recv()
    r1 = []
    for s in S:
        arrive(a2[s])
        c1 = project(s, 0, ag, wo)
        r1.append(scatter_z(s, 0, c1))
    share_wd = send(wd_hbm.at[sib_units], wd.at[1], wss.at[3], wrs.at[3], sibling)
    for copy in (load_wg, load_wu, load_wd):
        copy.wait()
    for copy in (share_gain, share_wg, share_wu):
        copy.wait_recv()
    drain(16)
    r1 = [relay_z(s, 0, r1[s]) for s in S]
    n1 = [norm_gather(s, r1[s]) for s in S]
    n1 = [relay_normed(s, n1[s]) for s in S]
    drain(32)
    share_wd.wait_recv()
    squares(0, swap_normed(0, n1[0]))
    expand(0, 0)
    e1 = {(0, 0): scatter_first(0, 0)}
    expand(0, 1)
    e1[0, 1] = scatter_first(0, 1)
    squares(1, swap_normed(1, n1[1]))
    drain(40)
    e2, f1, f2 = {}, {}, {}
    e1[0, 0] = relay(0, 0, e1[0, 0])
    expand(1, 0)
    e1[0, 1] = relay(0, 1, e1[0, 1])
    e1[1, 0] = scatter_first(1, 0)
    expand(1, 1)
    e2[0, 0] = scatter_second(0, 0, e1[0, 0])
    e1[1, 1] = scatter_first(1, 1)
    e2[0, 1] = scatter_second(0, 1, e1[0, 1])
    e1[1, 0] = relay(1, 0, e1[1, 0])
    f1[0, 0] = activate(0, 0, e2[0, 0])
    e1[1, 1] = relay(1, 1, e1[1, 1])
    f1[0, 1] = activate(0, 1, e2[0, 1])
    e2[1, 0] = scatter_second(1, 0, e1[1, 0])
    f2[0, 0] = gather_on(0, 0, f1[0, 0])
    e2[1, 1] = scatter_second(1, 1, e1[1, 1])
    f2[0, 1] = gather_on(0, 1, f1[0, 1])
    f1[1, 0] = activate(1, 0, e2[1, 0])
    f2[0, 0] = forward(0, 8, ac[0], f2[0, 0])
    f1[1, 1] = activate(1, 1, e2[1, 1])
    f2[0, 1] = forward(0, 9, ac[1], f2[0, 1])
    f2[1, 0] = gather_on(1, 0, f1[1, 0])
    f2[1, 1] = gather_on(1, 1, f1[1, 1])
    down(0, 0, f2[0, 0])
    c2 = down(0, 1, f2[0, 1])
    f2[1, 0] = forward(1, 8, ac[0], f2[1, 0])
    r2 = [scatter_z(0, 1, c2)]
    f2[1, 1] = forward(1, 9, ac[1], f2[1, 1])
    drain(len(sent) - 40)
    down(1, 0, f2[1, 0])
    r2[0] = relay_z(0, 1, r2[0])
    c2 = down(1, 1, f2[1, 1])
    r2.append(scatter_z(1, 1, c2))
    drain(len(sent) - 16)
    r2[1] = relay_z(1, 1, r2[1])
    for s in S:
        fin[s] = st[s] + sum_z(s, 1, r2[s])
    for g in range(share // 8):
        out_ref[g * 16:(g + 1) * 16, :] = jnp.concatenate(
            [fin[s, g * 8:(g + 1) * 8, :] for s in S], axis=0
        ).astype(BF16)
    drain(len(sent))


def local(
    queries, cache_keys, cache_values, new_key, new_value, lengths,
    out_weight, residual, norm_gain, gate_weight, up_weight, down_weight,
):
    seqs, ctx, _ = cache_keys.shape
    heads = queries.shape[1] // HD
    half = seqs // STREAMS
    kh = out_weight.shape[0] // 2
    cols = out_weight.shape[1]
    depth, hidden = gate_weight.shape
    units = hidden // 2
    cut = units // 256 * 128
    w0, w1 = 2 * cut + 128, 2 * (units - cut)
    rows = NX * NY * 2 * half
    share = rows // NZ
    S = STREAMS
    DMA = pltpu.SemaphoreType.DMA

    def v(*shape, dtype=BF16):
        return pltpu.VMEM(shape, dtype)

    scratch = [
        v(*queries.shape), v(*new_key.shape), v(*new_value.shape), v(*residual.shape),
        v(1, cols, dtype=F32),
        v(seqs, ctx, HD), v(seqs, ctx, HD),
        v(2, kh, cols), v(2 * depth, units), v(2 * depth, units), v(2, units, cols),
        v(1, cols, dtype=F32),
        v(seqs * heads, HD, dtype=F32),
        v(S, half * heads, HD, dtype=F32),
        v(S, 2, half, kh, dtype=F32), v(S, half, kh, dtype=F32),
        v(S, NY, NX, 16, kh),
        v(S, 2, rows, cols, dtype=F32),
        v(S, 2, rows, cols), v(S, 2, rows, cols),
        v(S, 2, NZ, share, cols), v(S, 2, 8, share, cols),
        v(S, 2, 2, share, cols),
        v(S, share, cols, dtype=F32),
        v(S, NZ, share, 2 * depth), v(rows, 128, dtype=F32),
        v(S, NX, NY, 16, cut + 128), v(S, NX, NY, 16, units - cut),
        v(S, NX, NY, 16, cut), v(S, NX, NY, 16, units - cut),
        v(S, 3, NY, 16, cut + 128), v(S, 3, NY, 16, units - cut),
        v(S, 3, NY, 16, cut), v(S, 3, NY, 16, units - cut),
        v(S, NY, 16, cut + 128), v(S, NY, 16, units - cut),
        v(S, NY, 16, cut), v(S, NY, 16, units - cut),
        v(S, NY, 16, w0), v(S, NY, 16, w1),
        v(S, 3, 16, w0), v(S, 3, 16, w1),
        v(S, NY, NX, 16, cut), v(S, NY, NX, 16, units - cut),
        v(rows, cols, dtype=F32), v(S, 16, 128, dtype=F32),
        v(S, share, cols, dtype=F32),
        DMA((13,)), DMA((5,)), DMA((5,)),
        DMA((S, 4)), DMA((S, 4)),
        DMA((S, 10, 6)), DMA((S, 10, 6)),
        DMA((S, 3, 8)), DMA((S, 3, 8)),
    ]
    vm = pl.BlockSpec(memory_space=pltpu.VMEM)
    hbm = pl.BlockSpec(memory_space=pl.ANY)
    return pl.pallas_call(
        body,
        out_shape=jax.ShapeDtypeStruct(residual.shape, BF16),
        in_specs=[pl.BlockSpec(memory_space=pltpu.SMEM)] + [hbm] * 11,
        out_specs=vm,
        scratch_shapes=scratch,
        compiler_params=pltpu.CompilerParams(
            collective_id=0, has_side_effects=True, vmem_limit_bytes=58 << 20
        ),
        name="layer",
    )(
        lengths, queries, new_key, new_value, residual, norm_gain.reshape(1, -1),
        cache_keys, cache_values, out_weight, gate_weight, up_weight, down_weight,
    )


def solution(mesh):
    in_specs = (
        P("wide", "narrow"),
        P("wide", None, "narrow"),
        P("wide", None, "narrow"),
        P("wide", "narrow"),
        P("wide", "narrow"),
        P("wide"),
        P("narrow", "wide"),
        P("narrow", "wide"),
        P("wide"),
        P("wide", "narrow"),
        P("wide", "narrow"),
        P("narrow", "wide"),
    )
    out_specs = P("narrow", "wide")
    return jax.shard_map(local, mesh=mesh, in_specs=in_specs, out_specs=out_specs, check_vma=False)
```

```python
import functools
import math

import jax
import jax.numpy as jnp
from jax import lax
from jax.experimental import pallas as pl
from jax.experimental.pallas import tpu as pltpu
from jax.sharding import PartitionSpec as P

D = 16384
HD = 128
EPS = 1e-05
NX, NY, NZ = 4, 4, 8
STREAMS = 2
MESH = pl.DeviceIdType.MESH
F32 = jnp.float32
BF16 = jnp.bfloat16


def body(
    len_ref, q_hbm, nk_hbm, nv_hbm, res_hbm, gain_hbm,
    k_hbm, v_hbm, wo_hbm, wg_hbm, wu_hbm, wd_hbm,
    out_ref,
    q_ref, nk_ref, nv_ref, res_ref, gain_ref, kv, vv, wo, wg, wu, wd, gain_sib, qs, ao, ps, pr, ag, po, cs, cr, zs, zr, zt, st,
    xn, sq, ga0, ga1, gb0, gb1, ra0, ra1, rb0, rb1, ha0, ha1, hb0, hb1, gp0, gp1, gr20, gr21, ac0, ac1, psum, scales, fin,
    lsem, wss, wrs, d2s, d2r, p4s, p4r, zss, zrs,
):
    ga, gb, ra, rb = (ga0, ga1), (gb0, gb1), (ra0, ra1), (rb0, rb1)
    ha, hb, gp, gr2, ac = (ha0, ha1), (hb0, hb1), (gp0, gp1), (gr20, gr21), (ac0, ac1)
    w = lax.axis_index("wide")
    z = lax.axis_index("narrow")
    c = lax.rem(w, 2)
    chip = lax.div(w, 2)
    x = lax.rem(chip, NX)
    y = lax.div(chip, NX)
    units = wg.shape[1]
    depth = wg.shape[0] // 2

    sibling = (chip * 2 + (1 - c), z)

    p = jnp.where(c == 0, x, y)
    q = jnp.where(c == 0, y, x)

    def natural(second, first):
        return jnp.where(c == 0, second * NX + first, first * NX + second)

    def ppeer(d):
        return lax.rem(p + d, NX)

    def qpeer(d):
        return lax.rem(q + d, NX)

    def zpeer(d):
        return lax.rem(z + d, NZ)

    def pdev(d):
        return (natural(q, ppeer(d)) * 2 + c, z)

    def qdev(d):
        return (natural(qpeer(d), p) * 2 + c, z)

    def zdev(d):
        return (w, zpeer(d))

    barrier = pltpu.get_barrier_semaphore()
    peers = [sibling] + [pdev(d) for d in (1, 2, 3)] + [qdev(d) for d in (1, 2, 3)]
    peers += [zdev(d) for d in range(1, NZ)]
    for dev in peers:
        pl.semaphore_signal(barrier, inc=1, device_id=dev, device_id_type=MESH)

    sent = []
    drained = []

    def send(src, dst, ss, rs, dev):
        copy = pltpu.make_async_remote_copy(
            src_ref=src, dst_ref=dst, send_sem=ss, recv_sem=rs, device_id=dev, device_id_type=MESH
        )
        copy.start()
        sent.append(copy)
        return copy

    def drain(count):
        while len(drained) < count:
            copy = sent[len(drained)]
            copy.wait_send()
            drained.append(copy)

    k_rows = wo.shape[1]
    f_rows = wd.shape[1]
    d_cols = pl.ds(pl.multiple_of(c * units, 128), units)
    d_cols_sib = pl.ds(pl.multiple_of((1 - c) * units, 128), units)
    half = kv.shape[0] // STREAMS
    small = [
        pltpu.make_async_copy(src, dst, lsem.at[8 + i])
        for i, (src, dst) in enumerate((
            (q_hbm, q_ref), (nk_hbm, nk_ref), (nv_hbm, nv_ref), (res_hbm, res_ref),
            (gain_hbm, gain_ref),
        ))
    ]
    loads = []
    for s in range(STREAMS):
        rows = pl.ds(s * half, half)
        loads.append(pltpu.make_async_copy(k_hbm.at[rows], kv.at[rows], lsem.at[2 * s]))
        loads.append(pltpu.make_async_copy(v_hbm.at[rows], vv.at[rows], lsem.at[2 * s + 1]))
    own_rows = pl.ds(pl.multiple_of(c * k_rows, 128), k_rows)
    sib_rows = pl.ds(pl.multiple_of((1 - c) * k_rows, 128), k_rows)
    own_units = pl.ds(pl.multiple_of(c * f_rows, 128), f_rows)
    sib_units = pl.ds(pl.multiple_of((1 - c) * f_rows, 128), f_rows)
    load_wo = pltpu.make_async_copy(wo_hbm.at[own_rows], wo.at[0], lsem.at[4])
    load_wg = pltpu.make_async_copy(wg_hbm.at[:, d_cols], wg.at[0:depth], lsem.at[5])
    load_wu = pltpu.make_async_copy(wu_hbm.at[:, d_cols], wu.at[0:depth], lsem.at[6])
    load_wd = pltpu.make_async_copy(wd_hbm.at[own_units], wd.at[0], lsem.at[7])
    for copy in small + loads + [load_wo, load_wg, load_wu, load_wd]:
        copy.start()

    for copy in small:
        copy.wait()
    heads = q_ref.shape[1] // HD
    seqs = q_ref.shape[0]
    for h in range(heads):
        qs[pl.ds(h, seqs, stride=heads), :] = q_ref[:, h * HD:(h + 1) * HD].astype(F32)

    scale = 1.0 / math.sqrt(HD)

    def attend(s):
        loads[2 * s].wait()
        loads[2 * s + 1].wait()
        ctx = kv.shape[1]
        position = lax.broadcasted_iota(jnp.int32, (heads, ctx), 1)
        items = range(half)
        seq = [s * half + i for i in items]
        query = [qs[n * heads:(n + 1) * heads, :] for n in seq]
        score = [
            lax.dot_general(
                query[i].astype(BF16), kv[seq[i]], (((1,), (1,)), ((), ())),
                preferred_element_type=F32,
            )
            for i in items
        ]
        own = [
            jnp.sum(query[i] * nk_ref[n:n + 1, :].astype(F32), axis=1, keepdims=True) * scale
            for i, n in enumerate(seq)
        ]
        live = [position < len_ref[n] for n in seq]
        score = [jnp.where(live[i], score[i] * scale, -1e30) for i in items]
        top = [jnp.maximum(jnp.max(score[i], axis=1, keepdims=True), own[i]) for i in items]
        raw = [jnp.where(live[i], jnp.exp(score[i] - top[i]), 0.0) for i in items]
        own_raw = [jnp.exp(own[i] - top[i]) for i in items]
        inverse = [1.0 / (jnp.sum(raw[i], axis=1, keepdims=True) + own_raw[i]) for i in items]
        weights = [(raw[i] * inverse[i]).astype(BF16) for i in items]
        own_weight = [(own_raw[i] * inverse[i]).astype(BF16).astype(F32) for i in items]
        mixed = [jnp.dot(weights[i], vv[seq[i]], preferred_element_type=F32) for i in items]
        for i, n in enumerate(seq):
            ao[s, i * heads:(i + 1) * heads, :] = (
                mixed[i] + own_weight[i] * nv_ref[n:n + 1, :].astype(F32)
            )

    per_core = heads // 2

    def swap_start(s):
        for h in range(per_core):
            cols = slice(h * HD, (h + 1) * HD)
            ps[s, 0, :, cols] = ao[s, pl.ds(c * per_core + h, half, stride=heads), :]
            ps[s, 1, :, cols] = ao[s, pl.ds((1 - c) * per_core + h, half, stride=heads), :]
        return send(ps.at[s, 1], pr.at[s], d2s.at[s, 0], d2r.at[s, 0], sibling)

    def gather_first(s, k, buf):
        return [
            send(buf.at[s, q, p], buf.at[s, q, p], p4s.at[s, k, d - 1], p4r.at[s, k, d - 1], pdev(d))
            for d in (2, 1, 3)
        ]

    def gather_second(s, k, buf):
        return [
            send(buf.at[s, q], buf.at[s, q], p4s.at[s, k, d - 1], p4r.at[s, k, d - 1], qdev(d))
            for d in (2, 1, 3)
        ]

    low, high = slice(0, NX // 2), slice(NX // 2, NX)

    def gather_around(s, k, buf):
        return [
            send(buf.at[s, q, part], buf.at[s, q, part], p4s.at[s, k, i], p4r.at[s, k, i], qdev(d))
            for i, (part, d) in enumerate(((low, 1), (high, 3), (high, 1), (low, 3)))
        ]

    def forward(s, k, buf, copies):
        for i, (part, d) in enumerate(((low, 1), (high, 3))):
            copies[i].wait_recv()
            block = buf.at[s, qpeer(4 - d), part]
            copies.append(send(block, block, p4s.at[s, k, 4 + i], p4r.at[s, k, 4 + i], qdev(d)))
        return copies[2:]

    def arrive(copies):
        for copy in copies:
            copy.wait_recv()

    def swap_end_gather(s, copy):
        copy.wait_recv()
        mine = ps[s, 0]
        theirs = pr[s]
        first = jnp.where(c == 0, mine, theirs)
        second = jnp.where(c == 0, theirs, mine)
        block = jnp.concatenate([first, second], axis=0).astype(BF16)
        ag[s, q, p] = block
        return gather_first(s, 0, ag)

    rows = NX * NY * 16

    def project(s, k, buf, weight, first=0, last=True):
        depth_here = buf.shape[-1]
        copy = None
        for half_index in (1, 0):
            for n in range(weight.shape[-1] // 256):
                cols = slice(n * 256, (n + 1) * 256)
                acc = jnp.dot(buf[s].reshape(rows, depth_here),
                              weight[half_index, first:first + depth_here, cols],
                              preferred_element_type=F32)
                for a in range(NY):
                    for b in range(NX):
                        r = (a * NX + b) * 16
                        to = pl.ds(pl.multiple_of(natural(a, b) * 16, 16), 16)
                        value = acc[r:r + 16]
                        held = psum if half_index else po.at[s, k]
                        if first:
                            value = value + held[to, cols]
                        if half_index and last:
                            cs[s, k, to, cols] = value.astype(BF16)
                        else:
                            held[to, cols] = value
            if half_index and last:
                copy = send(cs.at[s, k], cr.at[s, k], d2s.at[s, 1 + k], d2r.at[s, 1 + k], sibling)
        return copy

    share = rows // NZ
    top, bottom = slice(0, share // 2), slice(share // 2, share)

    def zsend(s, k, i, src, dst, d):
        return send(src, dst, zss.at[s, k, i], zrs.at[s, k, i], zdev(d))

    def scatter_z(s, k, copy):
        copy.wait_recv()
        for j in range(NZ):
            r = slice(j * share, (j + 1) * share)
            zs[s, k, j] = (po[s, k, r, :] + cr[s, k, r, :].astype(F32)).astype(BF16)
        src = [zs.at[s, k, zpeer(d)] for d in range(NZ)]
        return [
            zsend(s, k, 0, src[4].at[top], zr.at[s, k, 0, top], 2),
            zsend(s, k, 1, src[4].at[bottom], zr.at[s, k, 1, bottom], 6),
            zsend(s, k, 2, src[3], zr.at[s, k, 2], 1),
            zsend(s, k, 3, src[5], zr.at[s, k, 3], 7),
            zsend(s, k, 4, src[1], zr.at[s, k, 4], 1),
            zsend(s, k, 5, src[7], zr.at[s, k, 5], 7),
        ]

    def relay_z(s, k, copies):
        for i, (part, d) in enumerate(((top, 2), (bottom, 6))):
            copies[i].wait_recv()
            copies[2 + i].wait_recv()
            to = zpeer(d)
            zt[s, k, i] = (zs[s, k, to].astype(F32) + zr[s, k, 2 + i].astype(F32)).astype(BF16)
            zt[s, k, i, part] = (
                zs[s, k, to, part].astype(F32) + zr[s, k, 2 + i, part].astype(F32)
                + zr[s, k, i, part].astype(F32)
            ).astype(BF16)
            copies.append(zsend(s, k, 6 + i, zt.at[s, k, i], zr.at[s, k, 6 + i], d))
        return copies[4:]

    def sum_z(s, k, copies):
        own = pl.ds(pl.multiple_of(z * share, share), share)
        acc = po[s, k, own, :] + cr[s, k, own, :].astype(F32)
        arrive(copies)
        for i in range(4, 8):
            acc += zr[s, k, i].astype(F32)
        return acc

    def norm_gather(s, copies):
        stream = sum_z(s, 0, copies)
        pieces = [
            res_ref[g * 16:(g + 1) * 16, :].astype(F32)[s * 8:(s + 1) * 8] for g in range(share // 8)
        ]
        stream = stream + jnp.concatenate(pieces, axis=0)
        st[s] = stream
        xn[s, z, :, 0:depth] = (stream * gain_ref[...]).astype(BF16)
        block = xn.at[s, z, :, 0:depth]
        return [zsend(s, 2, i, block, block, d) for i, d in enumerate((2, 6, 1, 7))]

    def relay_normed(s, copies):
        for i, (part, near, far) in enumerate(((top, 1, 2), (bottom, 7, 6))):
            copies[i].wait_recv()
            came = zpeer(NZ - far)
            half_block = xn.at[s, came, part, 0:depth]
            block = xn.at[s, came, :, 0:depth]
            copies.append(zsend(s, 2, 4 + 2 * i, half_block, half_block, far))
            copies.append(zsend(s, 2, 5 + 2 * i, block, block, near))
        return copies[2:]

    def encode(value):
        high = value.astype(BF16).astype(F32)
        lane = lax.broadcasted_iota(jnp.int32, value.shape, 1)
        return jnp.where(lane < 64, high, value - high).astype(BF16)

    def decode(pair):
        value = pair.astype(F32)
        return value + pltpu.roll(value, 64, 1)

    def row_squares(s, first):
        gain = gain_sib if first else gain_ref
        ungain = 1.0 / gain[...]
        for j in range(NZ):
            value = xn[s, j, :, first:first + depth].astype(F32) * ungain
            value = value * value
            total = value[:, 0:128]
            for n in range(1, depth // 128):
                total += value[:, n * 128:(n + 1) * 128]
            r = slice(j * share, (j + 1) * share)
            if first:
                total += sq[r, :]
                total = jnp.broadcast_to(jnp.sum(total, axis=1, keepdims=True), (share, 128))
            sq[r, :] = total

    def swap_normed(s, copies):
        arrive(copies)
        return send(xn.at[s, :, :, 0:depth], xn.at[s, :, :, depth:2 * depth],
                    d2s.at[s, 3], d2r.at[s, 3], sibling)

    parts = [(0, ac[0].shape[-1]), (ac[0].shape[-1], ac[1].shape[-1])]

    def spread(buf, s, cols, value):
        for j in range(NY):
            for i in range(NX):
                r = (j * NX + i) * 16
                first = jnp.where(c == 0, i, j)
                second = jnp.where(c == 0, j, i)
                buf[s, first, second, :, cols] = value[r:r + 16]

    def expand(s, part, which=(0, 1)):
        base, count = parts[part]
        for k in which:
            weight, buf = ((wg, ga[part]), (wu, gb[part]))[k]
            for start in range(0, count, 256):
                size = min(256, count - start)
                acc = jnp.dot(xn[s].reshape(rows, 2 * depth),
                              weight[:, base + start:base + start + size],
                              preferred_element_type=F32)
                spread(buf, s, slice(start, start + size), acc.astype(BF16))

    def plane_send(s, part, i, src, dst, d):
        return send(src, dst, p4s.at[s, 2 + part, i], p4r.at[s, 2 + part, i], pdev(d))

    def scatter_first(s, part):
        first = scatter_gate(s, part)
        second = scatter_up(s, part)
        return [first[0], second[0], first[1], second[1]]

    def scatter_gate(s, part):
        a, ta = ga[part], ra[part]
        return [
            plane_send(s, part, 0, a.at[s, ppeer(2)], ta.at[s, 0], 1),
            plane_send(s, part, 2, a.at[s, ppeer(3)], ta.at[s, 1], 3),
        ]

    def scatter_up(s, part):
        b, tb = gb[part], rb[part]
        return [
            plane_send(s, part, 1, b.at[s, ppeer(2)], tb.at[s, 0], 3),
            plane_send(s, part, 3, b.at[s, ppeer(1)], tb.at[s, 1], 1),
        ]

    def add_rows(terms, count, out, base, squares_too):
        def block(j, _):
            blocks = [get(j) for get in terms]
            acc = blocks[0][:, 0:count].astype(F32)
            for value in blocks[1:]:
                acc += value[:, 0:count].astype(F32)
            out[j, :, base:base + count] = acc.astype(BF16)
            if squares_too:
                square = decode(blocks[0][:, count:])
                for value in blocks[1:]:
                    square += decode(value[:, count:])
                end = out.shape[-1]
                out[j, :, end - 128:end] = encode(square)
            return 0
        lax.fori_loop(0, NY, block, 0)

    def relay(s, part, copies):
        a, b, ta, tb = ga[part], gb[part], ra[part], rb[part]
        count = parts[part][1]
        copies[0].wait_recv()
        add_rows([lambda j: a[s, ppeer(1), j], lambda j: ta[s, 0, j]], count,
                 ha[part].at[s], 0, part == 0)
        copies.append(plane_send(s, part, 4, ha[part].at[s], ta.at[s, 2], 1))
        copies[1].wait_recv()
        add_rows([lambda j: b[s, ppeer(3), j], lambda j: tb[s, 0, j]], count,
                 hb[part].at[s], 0, False)
        copies.append(plane_send(s, part, 5, hb[part].at[s], tb.at[s, 2], 3))
        return copies[2:]

    def scatter_second(s, part, copies):
        a, b, ta, tb = ga[part], gb[part], ra[part], rb[part]
        count = parts[part][1]
        arrive(copies)
        add_rows([lambda j: a[s, p, j], lambda j: ta[s, 1, j], lambda j: ta[s, 2, j]], count,
                 gp[part].at[s], 0, part == 0)
        add_rows([lambda j: b[s, p, j], lambda j: tb[s, 1, j], lambda j: tb[s, 2, j]], count,
                 gp[part].at[s], count, False)
        return [
            send(gp[part].at[s, qpeer(d)], gr2[part].at[s, d - 1],
                 p4s.at[s, 4 + part, d - 1], p4r.at[s, 4 + part, d - 1], qdev(d))
            for d in (2, 1, 3)
        ]

    def activate(s, part, copies):
        arrive(copies)
        count = parts[part][1]
        if part == 0:
            square = decode(gp[0][s, q, :, 2 * count:])
            for d in range(3):
                square += decode(gr2[0][s, d, :, 2 * count:])
            scales[s] = lax.rsqrt(square / D + EPS)
        factor = scales[s]
        for n in range(count // 128):
            cols = slice(n * 128, (n + 1) * 128)
            lift_cols = slice(count + n * 128, count + (n + 1) * 128)
            gate = gp[part][s, q, :, cols].astype(F32)
            lift = gp[part][s, q, :, lift_cols].astype(F32)
            for d in range(3):
                gate += gr2[part][s, d, :, cols].astype(F32)
                lift += gr2[part][s, d, :, lift_cols].astype(F32)
            gate = gate * factor
            ac[part][s, q, p, :, cols] = (
                gate / (1.0 + jnp.exp(-gate)) * (lift * factor)
            ).astype(BF16)
        return gather_first(s, 6 + part, ac[part])

    def gather_on(s, part, copies):
        arrive(copies)
        return gather_around(s, 8 + part, ac[part])

    def down(s, part, copies):
        arrive(copies)
        return project(s, 1, ac[part], wd, parts[part][0], part == 1)

    def squares(s, copy):
        row_squares(s, 0)
        copy.wait_recv()
        row_squares(s, depth)
        count = parts[0][1]
        spread(ga[0], s, slice(count, count + 128), encode(sq[...]))

    S = range(STREAMS)
    for s in S:
        attend(s)
    pl.semaphore_wait(barrier, len(peers))
    swaps = [swap_start(s) for s in S]
    share_gain = send(gain_hbm, gain_sib, wss.at[4], wrs.at[4], sibling)
    share_wo = send(wo_hbm.at[sib_rows], wo.at[1], wss.at[0], wrs.at[0], sibling)
    a1 = [swap_end_gather(s, swaps[s]) for s in S]
    share_wg = send(wg_hbm.at[:, d_cols_sib], wg.at[depth:2 * depth], wss.at[1], wrs.at[1], sibling)
    share_wu = send(wu_hbm.at[:, d_cols_sib], wu.at[depth:2 * depth], wss.at[2], wrs.at[2], sibling)
    a2 = []
    for s in S:
        arrive(a1[s])
        a2.append(gather_second(s, 1, ag))
    load_wo.wait()
    share_wo.wait_recv()
    r1 = []
    for s in S:
        arrive(a2[s])
        c1 = project(s, 0, ag, wo)
        r1.append(scatter_z(s, 0, c1))
    share_wd = send(wd_hbm.at[sib_units], wd.at[1], wss.at[3], wrs.at[3], sibling)
    for copy in (load_wg, load_wu, load_wd):
        copy.wait()
    for copy in (share_gain, share_wg, share_wu):
        copy.wait_recv()
    drain(16)
    r1 = [relay_z(s, 0, r1[s]) for s in S]
    n1 = [norm_gather(s, r1[s]) for s in S]
    n1 = [relay_normed(s, n1[s]) for s in S]
    drain(32)
    share_wd.wait_recv()
    squares(0, swap_normed(0, n1[0]))
    e1 = {}
    for part in (0, 1):
        expand(0, part, (0,))
        first = scatter_gate(0, part)
        expand(0, part, (1,))
        second = scatter_up(0, part)
        e1[0, part] = [first[0], second[0], first[1], second[1]]
    squares(1, swap_normed(1, n1[1]))
    drain(40)
    e2, f1, f2 = {}, {}, {}
    e1[0, 0] = relay(0, 0, e1[0, 0])
    expand(1, 0)
    e1[0, 1] = relay(0, 1, e1[0, 1])
    e1[1, 0] = scatter_first(1, 0)
    expand(1, 1)
    e2[0, 0] = scatter_second(0, 0, e1[0, 0])
    e1[1, 1] = scatter_first(1, 1)
    e2[0, 1] = scatter_second(0, 1, e1[0, 1])
    e1[1, 0] = relay(1, 0, e1[1, 0])
    f1[0, 0] = activate(0, 0, e2[0, 0])
    e1[1, 1] = relay(1, 1, e1[1, 1])
    f1[0, 1] = activate(0, 1, e2[0, 1])
    e2[1, 0] = scatter_second(1, 0, e1[1, 0])
    f2[0, 0] = gather_on(0, 0, f1[0, 0])
    e2[1, 1] = scatter_second(1, 1, e1[1, 1])
    f2[0, 1] = gather_on(0, 1, f1[0, 1])
    f1[1, 0] = activate(1, 0, e2[1, 0])
    f2[0, 0] = forward(0, 8, ac[0], f2[0, 0])
    f1[1, 1] = activate(1, 1, e2[1, 1])
    f2[0, 1] = forward(0, 9, ac[1], f2[0, 1])
    f2[1, 0] = gather_on(1, 0, f1[1, 0])
    f2[1, 1] = gather_on(1, 1, f1[1, 1])
    down(0, 0, f2[0, 0])
    c2 = down(0, 1, f2[0, 1])
    f2[1, 0] = forward(1, 8, ac[0], f2[1, 0])
    r2 = [scatter_z(0, 1, c2)]
    f2[1, 1] = forward(1, 9, ac[1], f2[1, 1])
    drain(len(sent) - 40)
    down(1, 0, f2[1, 0])
    r2[0] = relay_z(0, 1, r2[0])
    c2 = down(1, 1, f2[1, 1])
    r2.append(scatter_z(1, 1, c2))
    drain(len(sent) - 16)
    r2[1] = relay_z(1, 1, r2[1])
    for s in S:
        fin[s] = st[s] + sum_z(s, 1, r2[s])
    for g in range(share // 8):
        out_ref[g * 16:(g + 1) * 16, :] = jnp.concatenate(
            [fin[s, g * 8:(g + 1) * 8, :] for s in S], axis=0
        ).astype(BF16)
    drain(len(sent))


def local(
    queries, cache_keys, cache_values, new_key, new_value, lengths,
    out_weight, residual, norm_gain, gate_weight, up_weight, down_weight,
):
    seqs, ctx, _ = cache_keys.shape
    heads = queries.shape[1] // HD
    half = seqs // STREAMS
    kh = out_weight.shape[0] // 2
    cols = out_weight.shape[1]
    depth, hidden = gate_weight.shape
    units = hidden // 2
    cut = units // 256 * 128
    w0, w1 = 2 * cut + 128, 2 * (units - cut)
    rows = NX * NY * 2 * half
    share = rows // NZ
    S = STREAMS
    DMA = pltpu.SemaphoreType.DMA

    def v(*shape, dtype=BF16):
        return pltpu.VMEM(shape, dtype)

    scratch = [
        v(*queries.shape), v(*new_key.shape), v(*new_value.shape), v(*residual.shape),
        v(1, cols, dtype=F32),
        v(seqs, ctx, HD), v(seqs, ctx, HD),
        v(2, kh, cols), v(2 * depth, units), v(2 * depth, units), v(2, units, cols),
        v(1, cols, dtype=F32),
        v(seqs * heads, HD, dtype=F32),
        v(S, half * heads, HD, dtype=F32),
        v(S, 2, half, kh, dtype=F32), v(S, half, kh, dtype=F32),
        v(S, NY, NX, 16, kh),
        v(S, 2, rows, cols, dtype=F32),
        v(S, 2, rows, cols), v(S, 2, rows, cols),
        v(S, 2, NZ, share, cols), v(S, 2, 8, share, cols),
        v(S, 2, 2, share, cols),
        v(S, share, cols, dtype=F32),
        v(S, NZ, share, 2 * depth), v(rows, 128, dtype=F32),
        v(S, NX, NY, 16, cut + 128), v(S, NX, NY, 16, units - cut),
        v(S, NX, NY, 16, cut), v(S, NX, NY, 16, units - cut),
        v(S, 3, NY, 16, cut + 128), v(S, 3, NY, 16, units - cut),
        v(S, 3, NY, 16, cut), v(S, 3, NY, 16, units - cut),
        v(S, NY, 16, cut + 128), v(S, NY, 16, units - cut),
        v(S, NY, 16, cut), v(S, NY, 16, units - cut),
        v(S, NY, 16, w0), v(S, NY, 16, w1),
        v(S, 3, 16, w0), v(S, 3, 16, w1),
        v(S, NY, NX, 16, cut), v(S, NY, NX, 16, units - cut),
        v(rows, cols, dtype=F32), v(S, 16, 128, dtype=F32),
        v(S, share, cols, dtype=F32),
        DMA((13,)), DMA((5,)), DMA((5,)),
        DMA((S, 4)), DMA((S, 4)),
        DMA((S, 10, 6)), DMA((S, 10, 6)),
        DMA((S, 3, 8)), DMA((S, 3, 8)),
    ]
    vm = pl.BlockSpec(memory_space=pltpu.VMEM)
    hbm = pl.BlockSpec(memory_space=pl.ANY)
    return pl.pallas_call(
        body,
        out_shape=jax.ShapeDtypeStruct(residual.shape, BF16),
        in_specs=[pl.BlockSpec(memory_space=pltpu.SMEM)] + [hbm] * 11,
        out_specs=vm,
        scratch_shapes=scratch,
        compiler_params=pltpu.CompilerParams(
            collective_id=0, has_side_effects=True, vmem_limit_bytes=58 << 20
        ),
        name="layer",
    )(
        lengths, queries, new_key, new_value, residual, norm_gain.reshape(1, -1),
        cache_keys, cache_values, out_weight, gate_weight, up_weight, down_weight,
    )


def solution(mesh):
    in_specs = (
        P("wide", "narrow"),
        P("wide", None, "narrow"),
        P("wide", None, "narrow"),
        P("wide", "narrow"),
        P("wide", "narrow"),
        P("wide"),
        P("narrow", "wide"),
        P("narrow", "wide"),
        P("wide"),
        P("wide", "narrow"),
        P("wide", "narrow"),
        P("narrow", "wide"),
    )
    out_specs = P("narrow", "wide")
    return jax.shard_map(local, mesh=mesh, in_specs=in_specs, out_specs=out_specs, check_vma=False)
```
